32 devices in a mesh: orb: 8 (over y, x, core), grid: 4 (over z).
Axes of the slice: x: 2, y: 2, z: 4, core: 2. Of those that a mesh axis runs over, the one named last changes fastest.
Arguments:
- wavefunctions: float32 [64, 24, 1024], P('orb', 'grid'), may hold values from -2 to 2
- potential: float32 [24, 1024], P('grid'), may hold values from -3 to 0
Outputs:
- orbitals: float32 [64, 24, 1024], P('orb', 'grid')
The draws below stay inside these ranges and needn't reach their ends.
All inputs are finite; a program needn't handle non-finite values.
Results may differ from the reference program's by a relative error of at most 0.0003.
Values sent between devices are 32-bit elements; how exact they have to be, the bound alone decides.
No kernel may reach another device: no remote copies, remote signals or barrier semaphores. Data moves between devices by JAX's collectives and lax.ppermute only.
A program may use at most 64 MiB of HBM per device.

```python
import jax
import jax.numpy as jnp
from jax import lax

PANEL = 32
NPANEL = 2
NX = 32
NY = 32
NZ = 24
ORBS = 64


def block_levels(stream_key, extent, shards, least, high):
    factor_of, own = 1.0, jax.random.fold_in(stream_key, 6)
    for dim, parts in shards:
        steps = jnp.exp(jax.random.uniform(jax.random.fold_in(own, dim), (parts,), jnp.float32, least / len(shards), high / len(shards)))
        factor_of = factor_of * jnp.repeat(steps, extent[dim] // parts).reshape([-1 if axis == dim else 1 for axis in range(len(extent))])
    return factor_of


def centred(key, dims, width, reach, cuts=(), kind=jnp.bfloat16):
    drawn = jax.random.normal(key, dims, jnp.float32) * width
    if len(cuts) > 0:
        drawn = block_levels(key, dims, cuts, -0.22, 0.18) * drawn
    return jnp.clip(drawn, min=-reach, max=reach).astype(kind)


def setup_inputs(seed: int = 0) -> dict:
    splits = jax.random.split(jax.random.key(seed), 3)
    return {
        "wavefunctions": centred(splits[0], (ORBS, NZ, NX * NY), 0.25, 2.0, ((0, 8), (1, 4)), jnp.float32),
        "potential": jnp.clip(-3.0 + 3.0 * jax.random.uniform(splits[1], (NZ, NX * NY), jnp.float32) ** block_levels(splits[1], (NZ, NX * NY), ((0, 4),), -0.2, 0.2), -3.0, 0.0),
    }


COEFFS = (-5369.0 / 1800.0, 12.0 / 7.0, -15.0 / 56.0, 10.0 / 189.0, -1.0 / 112.0, 2.0 / 1925.0, -1.0 / 16632.0)
HIGH = lax.Precision.HIGHEST

def hamiltonian(args):
    block, potential = args
    count = block.shape[0]
    grid = block.reshape(count, NZ, NX, NY)
    padded = jnp.pad(grid, ((0, 0), (0, 0), (6, 6), (6, 6)))
    total = 3.0 * COEFFS[0] * grid
    for k in range(1, 7):
        total = total + COEFFS[k] * (jnp.roll(grid, -k, 1) + jnp.roll(grid, k, 1) + padded[:, :, 6 + k:6 + k + NX, 6:6 + NY] + padded[:, :, 6 - k:6 - k + NX, 6:6 + NY] + padded[:, :, 6:6 + NX, 6 + k:6 + k + NY] + padded[:, :, 6:6 + NX, 6 - k:6 - k + NY])
    result = -0.5 * total.reshape(count, NZ * NX * NY) + (potential[None] * block).reshape(count, NZ * NX * NY)
    return result

def reference(wavefunctions, potential):
    scale = 1.0 / (NZ * NX * NY)
    nblocks = ORBS // PANEL
    blocks = wavefunctions.reshape(nblocks, PANEL, NZ, NX * NY)
    blocks = lax.map(lambda blk: hamiltonian((blk, potential)), blocks)
    for p in range(NPANEL):
        current = blocks[p]
        gram = jnp.einsum('ic,jc->ij', current, current, precision=HIGH) * scale
        lower = jnp.linalg.cholesky(gram)
        ortho = lax.linalg.triangular_solve(lower, current, left_side=True, lower=True)

        def project(args):
            blk, index = args
            coeff = jnp.einsum('ic,jc->ij', ortho, blk, precision=HIGH) * scale
            moved = blk - jnp.einsum('ij,ic->jc', coeff, ortho, precision=HIGH)
            return jnp.where(index > p, moved, jnp.where(index == p, ortho, blk))
        blocks = lax.map(project, (blocks, jnp.arange(nblocks, dtype=jnp.int32)))
    return blocks.reshape(ORBS, NZ, NX * NY)
```

```python
import functools

import jax
import jax.numpy as jnp
from jax import lax
from jax.experimental import pallas as pl
from jax.experimental.pallas import tpu as pltpu
from jax.sharding import PartitionSpec as P

PANEL = 32
NPANEL = 2
NY = 32

COEFFS = (
    -5369.0 / 1800.0,
    12.0 / 7.0,
    -15.0 / 56.0,
    10.0 / 189.0,
    -1.0 / 112.0,
    2.0 / 1925.0,
    -1.0 / 16632.0,
)
HIGH = lax.Precision.HIGHEST
RIM = 6
LANES = 128


def local_kernel(v_ref, pot_ref, out_ref):
    depth, count, plane = v_ref.shape
    lane = lax.broadcasted_iota(jnp.int32, (count, plane), 1)
    column = lane % NY
    for p in range(depth):
        here = v_ref[p]
        acc = (-1.5 * COEFFS[0] + pot_ref[p : p + 1, :]) * here
        for k in range(1, RIM + 1):
            up, down = NY * k, plane - NY * k
            near = jnp.where(lane < down, pltpu.roll(here, down, 1), 0.0)
            near += jnp.where(lane >= up, pltpu.roll(here, up, 1), 0.0)
            near += jnp.where(column + k < NY, pltpu.roll(here, plane - k, 1), 0.0)
            near += jnp.where(column >= k, pltpu.roll(here, k, 1), 0.0)
            if p + k < depth:
                near += v_ref[p + k]
            if p >= k:
                near += v_ref[p - k]
            acc += (-0.5 * COEFFS[k]) * near
        out_ref[:, p * plane : (p + 1) * plane] = acc


def couple_kernel(local_ref, before_ref, after_ref, out_ref):
    rim, count, plane = before_ref.shape
    depth = out_ref.shape[1] // plane
    for p in range(depth):
        acc = local_ref[:, p * plane : (p + 1) * plane]
        for q in range(rim):
            if p + rim - q <= rim:
                acc += (-0.5 * COEFFS[p + rim - q]) * before_ref[q]
            if depth + q - p <= rim:
                acc += (-0.5 * COEFFS[depth + q - p]) * after_ref[q]
        out_ref[:, p * plane : (p + 1) * plane] = acc


def gram_kernel(scale, rank_ref, *refs):
    blocks, (gram_ref, stack_ref) = refs[:-2], refs[-2:]
    count = blocks[0].shape[0]
    total = count * len(blocks)
    rank = rank_ref[0]
    odd = rank % 2 == 1
    for k in range(0, len(blocks), 2):
        one, two = blocks[k][...], blocks[k + 1][...]
        pair = jnp.concatenate([jnp.where(odd, two, one), jnp.where(odd, one, two)], 0)
        high = pair.astype(jnp.bfloat16)
        low = (pair - high.astype(jnp.float32)).astype(jnp.bfloat16)
        first = pl.multiple_of((rank // 2 ^ k // 2) * (2 * count), 2 * count)
        stack_ref[pl.ds(first, 2 * count), :] = high
        stack_ref[pl.ds(total + first, 2 * count), :] = low
    whole = stack_ref[...]
    products = lax.dot_general(
        whole, whole, (((1,), (1,)), ((), ())), preferred_element_type=jnp.float32
    )
    gram = products[:total] + products[total:]
    gram_ref[...] = (gram[:, :total] + gram[:, total:]) * scale


def invert_factor(gram):
    size = gram.shape[0]
    rows = 8
    ident = (
        lax.broadcasted_iota(jnp.int32, (size, size), 0)
        == lax.broadcasted_iota(jnp.int32, (size, size), 1)
    ).astype(jnp.float32)
    whole = jnp.concatenate([gram, ident], 1)
    tiles = [whole[i : i + rows] for i in range(0, size, rows)]
    sub = lax.broadcasted_iota(jnp.int32, (rows, 1), 0)
    pivots = []
    for j in range(size):
        t, s = divmod(j, rows)
        pivot = tiles[t][s : s + 1, j : j + 1]
        pivots.append(pivot)
        row = tiles[t][s : s + 1] / pivot
        for i in range(t, len(tiles)):
            column = tiles[i][:, j : j + 1]
            if i == t:
                column = jnp.where(sub > s, column, 0.0)
            tiles[i] = tiles[i] - column * row
    norm = lax.rsqrt(jnp.concatenate(pivots, 0))
    return jnp.concatenate(tiles, 0)[:, size:] * norm


def finish_kernel(rank_ref, *refs):
    parts, (stack_ref, out_ref, factor_ref) = refs[:-3], refs[-3:]
    depth, count, plane = out_ref.shape
    gram = parts[0][...]
    for part in parts[1:]:
        gram = gram + part[...]
    factor_ref[...] = invert_factor(gram)
    rows = factor_ref[pl.ds(pl.multiple_of(rank_ref[0] * count, count), count), :]
    high = rows.astype(jnp.bfloat16).astype(jnp.float32)
    low = rows - high
    left = jnp.concatenate(
        [jnp.concatenate([high, high], 1), jnp.concatenate([low, low], 1)], 0
    ).astype(jnp.bfloat16)
    for p in range(depth):
        both = jnp.dot(
            left, stack_ref[:, p * plane : (p + 1) * plane], preferred_element_type=jnp.float32
        )
        out_ref[p] = both[:count] + both[count:]


def call(kernel, out_shape, inputs, scratch=(), flops=0):
    in_specs = [
        pl.BlockSpec(memory_space=pltpu.SMEM if a.dtype == jnp.int32 else pltpu.VMEM)
        for a in inputs
    ]
    out_specs = jax.tree.map(lambda s: pl.BlockSpec(memory_space=pltpu.VMEM), out_shape)
    return pl.pallas_call(
        kernel,
        out_shape=out_shape,
        in_specs=in_specs,
        out_specs=out_specs,
        scratch_shapes=scratch,
        compiler_params=pltpu.CompilerParams(vmem_limit_bytes=32 * 2**20),
        cost_estimate=pl.CostEstimate(flops=flops, bytes_accessed=10**6, transcendentals=0),
    )(*inputs)


def rotation(peers, step):
    return [(i, (i + step) % peers) for i in range(peers)]


def exchange(peers, mask):
    return [(i, i ^ mask) for i in range(peers)]


def shape(*dims, dtype=jnp.float32):
    return jax.ShapeDtypeStruct(dims, dtype)


def grid_sum(part, grid):
    if grid > 4:
        return [lax.psum(part, "grid")]
    return [part] + [lax.ppermute(part, "grid", rotation(grid, k)) for k in range(1, grid)]


def gather_all(work, orb):
    blocks = []
    for chip in range(0, orb, 2):
        block = work if chip == 0 else lax.ppermute(work, "orb", exchange(orb, chip))
        blocks += [block, lax.ppermute(block, "orb", exchange(orb, 1))]
    return blocks


def gather_leading(work, rank, members):
    kept = [jnp.where(rank == m, work, jnp.zeros_like(work)) for m in range(members)]
    return lax.psum(kept, "orb")


def finish_leading(work, blocks, gram, rank, scale):
    count = work.shape[0]
    leading = jnp.concatenate(blocks, 0)
    total = leading.shape[0]
    inner = functools.partial(jnp.einsum, "ic,jc->ij", precision=HIGH)
    coeff = lax.psum(inner(work, leading) * scale, "grid")
    inverse = lax.linalg.triangular_solve(
        jnp.linalg.cholesky(gram), jnp.eye(total, dtype=gram.dtype), left_side=True, lower=True
    )
    first = jnp.minimum(rank * count, total - count)
    owned = lax.dynamic_slice_in_dim(inverse, first, count, 0)
    taken = jnp.dot(inner(coeff, inverse), inverse, precision=HIGH)
    member = rank * count < total
    rows = jnp.where(member, owned, -taken)
    return jnp.where(member, 0.0, work) + jnp.dot(rows, leading, precision=HIGH)


def per_device(wavefunctions, potential):
    planes = jnp.transpose(wavefunctions, (1, 0, 2))
    depth, count, plane = planes.shape
    cells = depth * plane
    orb, grid = lax.axis_size("orb"), lax.axis_size("grid")
    members = min(PANEL * NPANEL // count, orb)
    total = members * count
    scale = 1.0 / (cells * grid)
    before = lax.ppermute(planes[depth - RIM :], "grid", rotation(grid, 1))
    after = lax.ppermute(planes[:RIM], "grid", rotation(grid, -1))
    local = call(local_kernel, shape(count, cells), [planes, potential], flops=10**9)
    work = call(couple_kernel, shape(count, cells), [local, before, after])
    rank = lax.axis_index("orb").astype(jnp.int32)
    everyone = members == orb and orb & (orb - 1) == 0
    blocks = gather_all(work, orb) if everyone else gather_leading(work, rank, members)
    gram, stack = call(
        functools.partial(gram_kernel, scale),
        (shape(total, total), shape(2 * total, cells, dtype=jnp.bfloat16)),
        [rank.reshape(1) if everyone else jnp.zeros((1,), jnp.int32), *blocks],
    )
    parts = grid_sum(gram, grid)
    if not everyone:
        rest = finish_leading(work, blocks, sum(parts), rank, scale)
        return rest.reshape(count, depth, plane)
    done = call(
        finish_kernel,
        shape(depth, count, plane),
        [rank.reshape(1), *parts, stack],
        scratch=[pltpu.VMEM((total, total), jnp.float32)],
    )
    return jnp.transpose(done, (1, 0, 2))


def solution(mesh):
    return jax.shard_map(
        per_device,
        mesh=mesh,
        in_specs=(P("orb", "grid", None), P("grid", None)),
        out_specs=P("orb", "grid", None),
        check_vma=False,
    )
```

```python
import functools

import jax
import jax.numpy as jnp
from jax import lax
from jax.experimental import pallas as pl
from jax.experimental.pallas import tpu as pltpu
from jax.sharding import PartitionSpec as P

PANEL = 32
NPANEL = 2
NY = 32

COEFFS = (
    -5369.0 / 1800.0,
    12.0 / 7.0,
    -15.0 / 56.0,
    10.0 / 189.0,
    -1.0 / 112.0,
    2.0 / 1925.0,
    -1.0 / 16632.0,
)
HIGH = lax.Precision.HIGHEST
RIM = 6
LANES = 128


def local_kernel(v_ref, pot_ref, out_ref):
    depth, count, plane = v_ref.shape
    lane = lax.broadcasted_iota(jnp.int32, (count, plane), 1)
    column = lane % NY
    for p in range(depth):
        here = v_ref[p]
        acc = (-1.5 * COEFFS[0] + pot_ref[p : p + 1, :]) * here
        for k in range(1, RIM + 1):
            up, down = NY * k, plane - NY * k
            near = jnp.where(lane < down, pltpu.roll(here, down, 1), 0.0)
            near += jnp.where(lane >= up, pltpu.roll(here, up, 1), 0.0)
            near += jnp.where(column + k < NY, pltpu.roll(here, plane - k, 1), 0.0)
            near += jnp.where(column >= k, pltpu.roll(here, k, 1), 0.0)
            if p + k < depth:
                near += v_ref[p + k]
            if p >= k:
                near += v_ref[p - k]
            acc += (-0.5 * COEFFS[k]) * near
        out_ref[:, p * plane : (p + 1) * plane] = acc


def couple_kernel(local_ref, before_ref, after_ref, out_ref):
    rim, count, plane = before_ref.shape
    depth = out_ref.shape[1] // plane
    for p in range(depth):
        acc = local_ref[:, p * plane : (p + 1) * plane]
        for q in range(rim):
            if p + rim - q <= rim:
                acc += (-0.5 * COEFFS[p + rim - q]) * before_ref[q]
            if depth + q - p <= rim:
                acc += (-0.5 * COEFFS[depth + q - p]) * after_ref[q]
        out_ref[:, p * plane : (p + 1) * plane] = acc


def gram_kernel(scale, rank_ref, *refs):
    blocks, (gram_ref, stack_ref) = refs[:-2], refs[-2:]
    count = blocks[0].shape[0]
    total = count * len(blocks)
    rank = rank_ref[0]
    odd = rank % 2 == 1
    for k in range(0, len(blocks), 2):
        one, two = blocks[k][...], blocks[k + 1][...]
        pair = jnp.concatenate([jnp.where(odd, two, one), jnp.where(odd, one, two)], 0)
        high = pair.astype(jnp.bfloat16)
        low = (pair - high.astype(jnp.float32)).astype(jnp.bfloat16)
        first = pl.multiple_of((rank // 2 ^ k // 2) * (2 * count), 2 * count)
        stack_ref[pl.ds(first, 2 * count), :] = high
        stack_ref[pl.ds(total + first, 2 * count), :] = low
    whole = stack_ref[...]
    products = lax.dot_general(
        whole, whole, (((1,), (1,)), ((), ())), preferred_element_type=jnp.float32
    )
    gram = products[:total] + products[total:]
    gram_ref[...] = (gram[:, :total] + gram[:, total:]) * scale


def invert_factor(gram):
    size = gram.shape[0]
    rows = 8
    full = (rows, 2 * size)
    ident = (
        lax.broadcasted_iota(jnp.int32, (size, size), 0)
        == lax.broadcasted_iota(jnp.int32, (size, size), 1)
    ).astype(jnp.float32)
    whole = jnp.concatenate([gram, ident], 1)
    tiles = [whole[i : i + rows] for i in range(0, size, rows)]
    done = []
    for t in range(len(tiles)):
        later = range(t + 1, len(tiles))
        columns = {
            i: [
                jnp.broadcast_to(tiles[i][:, t * rows + a : t * rows + a + 1], full)
                for a in range(rows)
            ]
            for i in (t, *later)
        }
        line = [jnp.broadcast_to(tiles[t][a : a + 1], full) for a in range(rows)]
        pivot = [
            [jnp.broadcast_to(columns[t][b][a : a + 1], full) for b in range(a + 1)]
            for a in range(rows)
        ]
        factor = [[None] * rows for _ in range(rows)]
        inverse = []
        for a in range(rows):
            inverse.append(1.0 / pivot[a][a])
            for b in range(a + 1, rows):
                factor[b][a] = pivot[b][a] * inverse[a]
                line[b] = line[b] - factor[b][a] * line[a]
                for c in range(a + 1, b + 1):
                    pivot[b][c] = pivot[b][c] - factor[b][a] * pivot[c][a]
        done += [(line[a] * lax.rsqrt(pivot[a][a]))[:1] for a in range(rows)]
        solved = [line[a] * inverse[a] for a in range(rows)]
        for a in range(rows - 1, -1, -1):
            for b in range(a):
                solved[b] = solved[b] - factor[a][b] * solved[a]
        for i in later:
            terms = [columns[i][a] * solved[a] for a in range(rows)]
            while len(terms) > 1:
                terms = [terms[k] + terms[k + 1] for k in range(0, len(terms), 2)]
            tiles[i] = tiles[i] - terms[0]
    return jnp.concatenate(done, 0)[:, size:]


def finish_kernel(rank_ref, *refs):
    parts, (stack_ref, out_ref, factor_ref) = refs[:-3], refs[-3:]
    depth, count, plane = out_ref.shape
    gram = parts[0][...]
    for part in parts[1:]:
        gram = gram + part[...]
    factor_ref[...] = invert_factor(gram)
    rows = factor_ref[pl.ds(pl.multiple_of(rank_ref[0] * count, count), count), :]
    high = rows.astype(jnp.bfloat16).astype(jnp.float32)
    low = rows - high
    left = jnp.concatenate(
        [jnp.concatenate([high, high], 1), jnp.concatenate([low, low], 1)], 0
    ).astype(jnp.bfloat16)
    for p in range(depth):
        both = jnp.dot(
            left, stack_ref[:, p * plane : (p + 1) * plane], preferred_element_type=jnp.float32
        )
        out_ref[p] = both[:count] + both[count:]


def call(kernel, out_shape, inputs, scratch=(), flops=0):
    in_specs = [
        pl.BlockSpec(memory_space=pltpu.SMEM if a.dtype == jnp.int32 else pltpu.VMEM)
        for a in inputs
    ]
    out_specs = jax.tree.map(lambda s: pl.BlockSpec(memory_space=pltpu.VMEM), out_shape)
    return pl.pallas_call(
        kernel,
        out_shape=out_shape,
        in_specs=in_specs,
        out_specs=out_specs,
        scratch_shapes=scratch,
        compiler_params=pltpu.CompilerParams(vmem_limit_bytes=32 * 2**20),
        cost_estimate=pl.CostEstimate(flops=flops, bytes_accessed=10**6, transcendentals=0),
    )(*inputs)


def rotation(peers, step):
    return [(i, (i + step) % peers) for i in range(peers)]


def exchange(peers, mask):
    return [(i, i ^ mask) for i in range(peers)]


def shape(*dims, dtype=jnp.float32):
    return jax.ShapeDtypeStruct(dims, dtype)


def grid_sum(part, grid):
    if grid > 4:
        return [lax.psum(part, "grid")]
    return [part] + [lax.ppermute(part, "grid", rotation(grid, k)) for k in range(1, grid)]


def gather_all(work, orb):
    blocks = []
    for chip in range(0, orb, 2):
        block = work if chip == 0 else lax.ppermute(work, "orb", exchange(orb, chip))
        blocks += [block, lax.ppermute(block, "orb", exchange(orb, 1))]
    return blocks


def gather_leading(work, rank, members):
    kept = [jnp.where(rank == m, work, jnp.zeros_like(work)) for m in range(members)]
    return lax.psum(kept, "orb")


def finish_leading(work, blocks, gram, rank, scale):
    count = work.shape[0]
    leading = jnp.concatenate(blocks, 0)
    total = leading.shape[0]
    inner = functools.partial(jnp.einsum, "ic,jc->ij", precision=HIGH)
    coeff = lax.psum(inner(work, leading) * scale, "grid")
    inverse = lax.linalg.triangular_solve(
        jnp.linalg.cholesky(gram), jnp.eye(total, dtype=gram.dtype), left_side=True, lower=True
    )
    first = jnp.minimum(rank * count, total - count)
    owned = lax.dynamic_slice_in_dim(inverse, first, count, 0)
    taken = jnp.dot(inner(coeff, inverse), inverse, precision=HIGH)
    member = rank * count < total
    rows = jnp.where(member, owned, -taken)
    return jnp.where(member, 0.0, work) + jnp.dot(rows, leading, precision=HIGH)


def per_device(wavefunctions, potential):
    planes = jnp.transpose(wavefunctions, (1, 0, 2))
    depth, count, plane = planes.shape
    cells = depth * plane
    orb, grid = lax.axis_size("orb"), lax.axis_size("grid")
    members = min(PANEL * NPANEL // count, orb)
    total = members * count
    scale = 1.0 / (cells * grid)
    before = lax.ppermute(planes[depth - RIM :], "grid", rotation(grid, 1))
    after = lax.ppermute(planes[:RIM], "grid", rotation(grid, -1))
    local = call(local_kernel, shape(count, cells), [planes, potential], flops=10**9)
    work = call(couple_kernel, shape(count, cells), [local, before, after])
    rank = lax.axis_index("orb").astype(jnp.int32)
    everyone = members == orb and orb & (orb - 1) == 0
    blocks = gather_all(work, orb) if everyone else gather_leading(work, rank, members)
    gram, stack = call(
        functools.partial(gram_kernel, scale),
        (shape(total, total), shape(2 * total, cells, dtype=jnp.bfloat16)),
        [rank.reshape(1) if everyone else jnp.zeros((1,), jnp.int32), *blocks],
    )
    parts = grid_sum(gram, grid)
    if not everyone:
        rest = finish_leading(work, blocks, sum(parts), rank, scale)
        return rest.reshape(count, depth, plane)
    done = call(
        finish_kernel,
        shape(depth, count, plane),
        [rank.reshape(1), *parts, stack],
        scratch=[pltpu.VMEM((total, total), jnp.float32)],
    )
    return jnp.transpose(done, (1, 0, 2))


def solution(mesh):
    return jax.shard_map(
        per_device,
        mesh=mesh,
        in_specs=(P("orb", "grid", None), P("grid", None)),
        out_specs=P("orb", "grid", None),
        check_vma=False,
    )
```

```python
import functools

import jax
import jax.numpy as jnp
from jax import lax
from jax.experimental import pallas as pl
from jax.experimental.pallas import tpu as pltpu
from jax.sharding import PartitionSpec as P

PANEL = 32
NPANEL = 2
NY = 32

COEFFS = (
    -5369.0 / 1800.0,
    12.0 / 7.0,
    -15.0 / 56.0,
    10.0 / 189.0,
    -1.0 / 112.0,
    2.0 / 1925.0,
    -1.0 / 16632.0,
)
HIGH = lax.Precision.HIGHEST
RIM = 6
LANES = 128


def local_kernel(v_ref, pot_ref, out_ref):
    depth, count, plane = v_ref.shape
    lane = lax.broadcasted_iota(jnp.int32, (count, plane), 1)
    column = lane % NY
    for p in range(depth):
        here = v_ref[p]
        acc = (-1.5 * COEFFS[0] + pot_ref[p : p + 1, :]) * here
        for k in range(1, RIM + 1):
            up, down = NY * k, plane - NY * k
            near = jnp.where(lane < down, pltpu.roll(here, down, 1), 0.0)
            near += jnp.where(lane >= up, pltpu.roll(here, up, 1), 0.0)
            near += jnp.where(column + k < NY, pltpu.roll(here, plane - k, 1), 0.0)
            near += jnp.where(column >= k, pltpu.roll(here, k, 1), 0.0)
            if p + k < depth:
                near += v_ref[p + k]
            if p >= k:
                near += v_ref[p - k]
            acc += (-0.5 * COEFFS[k]) * near
        out_ref[:, p * plane : (p + 1) * plane] = acc


def couple_kernel(swap_ref, local_ref, one_ref, two_ref, out_ref):
    @pl.when(swap_ref[0] == 0)
    def _():
        couple(local_ref, one_ref, two_ref, out_ref)

    @pl.when(swap_ref[0] == 1)
    def _():
        couple(local_ref, two_ref, one_ref, out_ref)


def couple(local_ref, before_ref, after_ref, out_ref):
    rim, count, plane = before_ref.shape
    depth = out_ref.shape[1] // plane
    for p in range(depth):
        acc = local_ref[:, p * plane : (p + 1) * plane]
        for q in range(rim):
            if p + rim - q <= rim:
                acc += (-0.5 * COEFFS[p + rim - q]) * before_ref[q]
            if depth + q - p <= rim:
                acc += (-0.5 * COEFFS[depth + q - p]) * after_ref[q]
        out_ref[:, p * plane : (p + 1) * plane] = acc


def gram_kernel(scale, rank_ref, *refs):
    blocks, (gram_ref, stack_ref) = refs[:-2], refs[-2:]
    count = blocks[0].shape[0]
    total = count * len(blocks)
    rank = rank_ref[0]
    odd = rank % 2 == 1
    for k in range(0, len(blocks), 2):
        one, two = blocks[k][...], blocks[k + 1][...]
        pair = jnp.concatenate([jnp.where(odd, two, one), jnp.where(odd, one, two)], 0)
        high = pair.astype(jnp.bfloat16)
        low = (pair - high.astype(jnp.float32)).astype(jnp.bfloat16)
        first = pl.multiple_of((rank // 2 ^ k // 2) * (2 * count), 2 * count)
        stack_ref[pl.ds(first, 2 * count), :] = high
        stack_ref[pl.ds(total + first, 2 * count), :] = low
    whole = stack_ref[...]
    products = lax.dot_general(
        whole, whole, (((1,), (1,)), ((), ())), preferred_element_type=jnp.float32
    )
    gram = products[:total] + products[total:]
    gram_ref[...] = (gram[:, :total] + gram[:, total:]) * scale


def invert_factor(gram):
    size = gram.shape[0]
    rows = 8
    full = (rows, 2 * size)
    ident = (
        lax.broadcasted_iota(jnp.int32, (size, size), 0)
        == lax.broadcasted_iota(jnp.int32, (size, size), 1)
    ).astype(jnp.float32)
    whole = jnp.concatenate([gram, ident], 1)
    tiles = [whole[i : i + rows] for i in range(0, size, rows)]
    done = []
    for t in range(len(tiles)):
        later = range(t + 1, len(tiles))
        columns = {
            i: [
                jnp.broadcast_to(tiles[i][:, t * rows + a : t * rows + a + 1], full)
                for a in range(rows)
            ]
            for i in (t, *later)
        }
        line = [jnp.broadcast_to(tiles[t][a : a + 1], full) for a in range(rows)]
        pivot = [
            [jnp.broadcast_to(columns[t][b][a : a + 1], full) for b in range(a + 1)]
            for a in range(rows)
        ]
        factor = [[None] * rows for _ in range(rows)]
        inverse = []
        for a in range(rows):
            inverse.append(1.0 / pivot[a][a])
            for b in range(a + 1, rows):
                factor[b][a] = pivot[b][a] * inverse[a]
                line[b] = line[b] - factor[b][a] * line[a]
                for c in range(a + 1, b + 1):
                    pivot[b][c] = pivot[b][c] - factor[b][a] * pivot[c][a]
        done += [(line[a] * lax.rsqrt(pivot[a][a]))[:1] for a in range(rows)]
        solved = [line[a] * inverse[a] for a in range(rows)]
        for a in range(rows - 1, -1, -1):
            for b in range(a):
                solved[b] = solved[b] - factor[a][b] * solved[a]
        for i in later:
            terms = [columns[i][a] * solved[a] for a in range(rows)]
            while len(terms) > 1:
                terms = [terms[k] + terms[k + 1] for k in range(0, len(terms), 2)]
            tiles[i] = tiles[i] - terms[0]
    return jnp.concatenate(done, 0)[:, size:]


def finish_kernel(rank_ref, *refs):
    parts, (stack_ref, out_ref, factor_ref) = refs[:-3], refs[-3:]
    depth, count, plane = out_ref.shape
    gram = parts[0][...]
    for part in parts[1:]:
        gram = gram + part[...]
    factor_ref[...] = invert_factor(gram)
    rows = factor_ref[pl.ds(pl.multiple_of(rank_ref[0] * count, count), count), :]
    high = rows.astype(jnp.bfloat16).astype(jnp.float32)
    low = rows - high
    left = jnp.concatenate(
        [jnp.concatenate([high, high], 1), jnp.concatenate([low, low], 1)], 0
    ).astype(jnp.bfloat16)
    for p in range(depth):
        both = jnp.dot(
            left, stack_ref[:, p * plane : (p + 1) * plane], preferred_element_type=jnp.float32
        )
        out_ref[p] = both[:count] + both[count:]


def call(kernel, out_shape, inputs, scratch=(), flops=0):
    in_specs = [
        pl.BlockSpec(memory_space=pltpu.SMEM if a.dtype == jnp.int32 else pltpu.VMEM)
        for a in inputs
    ]
    out_specs = jax.tree.map(lambda s: pl.BlockSpec(memory_space=pltpu.VMEM), out_shape)
    return pl.pallas_call(
        kernel,
        out_shape=out_shape,
        in_specs=in_specs,
        out_specs=out_specs,
        scratch_shapes=scratch,
        compiler_params=pltpu.CompilerParams(vmem_limit_bytes=32 * 2**20),
        cost_estimate=pl.CostEstimate(flops=flops, bytes_accessed=10**6, transcendentals=0),
    )(*inputs)


def rotation(peers, step):
    return [(i, (i + step) % peers) for i in range(peers)]


def exchange(peers, mask):
    return [(i, i ^ mask) for i in range(peers)]


def shape(*dims, dtype=jnp.float32):
    return jax.ShapeDtypeStruct(dims, dtype)


def halo(planes, grid):
    depth = planes.shape[0]
    if grid == 4 and depth == RIM:
        one = lax.ppermute(planes, "grid", exchange(grid, 3))
        two = lax.ppermute(planes, "grid", exchange(grid, 1))
        return one, two, (lax.axis_index("grid") % 2).astype(jnp.int32).reshape(1)
    before = lax.ppermute(planes[depth - RIM :], "grid", rotation(grid, 1))
    after = lax.ppermute(planes[:RIM], "grid", rotation(grid, -1))
    return before, after, jnp.zeros((1,), jnp.int32)


def grid_sum(part, grid):
    if grid > 4:
        return [lax.psum(part, "grid")]
    masks = (1, 3, 2) if grid == 4 else range(1, grid)
    paired = grid & (grid - 1) == 0
    pairs = [exchange(grid, k) if paired else rotation(grid, k) for k in masks]
    return [part] + [lax.ppermute(part, "grid", pair) for pair in pairs]


def gather_all(work, orb):
    blocks = []
    for chip in range(0, orb, 2):
        block = work if chip == 0 else lax.ppermute(work, "orb", exchange(orb, chip))
        blocks += [block, lax.ppermute(block, "orb", exchange(orb, 1))]
    return blocks


def gather_leading(work, rank, members):
    kept = [jnp.where(rank == m, work, jnp.zeros_like(work)) for m in range(members)]
    return lax.psum(kept, "orb")


def finish_leading(work, blocks, gram, rank, scale):
    count = work.shape[0]
    leading = jnp.concatenate(blocks, 0)
    total = leading.shape[0]
    inner = functools.partial(jnp.einsum, "ic,jc->ij", precision=HIGH)
    coeff = lax.psum(inner(work, leading) * scale, "grid")
    inverse = lax.linalg.triangular_solve(
        jnp.linalg.cholesky(gram), jnp.eye(total, dtype=gram.dtype), left_side=True, lower=True
    )
    first = jnp.minimum(rank * count, total - count)
    owned = lax.dynamic_slice_in_dim(inverse, first, count, 0)
    taken = jnp.dot(inner(coeff, inverse), inverse, precision=HIGH)
    member = rank * count < total
    rows = jnp.where(member, owned, -taken)
    return jnp.where(member, 0.0, work) + jnp.dot(rows, leading, precision=HIGH)


def per_device(wavefunctions, potential):
    planes = jnp.transpose(wavefunctions, (1, 0, 2))
    depth, count, plane = planes.shape
    cells = depth * plane
    orb, grid = lax.axis_size("orb"), lax.axis_size("grid")
    members = min(PANEL * NPANEL // count, orb)
    total = members * count
    scale = 1.0 / (cells * grid)
    one, two, swap = halo(planes, grid)
    local = call(local_kernel, shape(count, cells), [planes, potential], flops=10**9)
    work = call(couple_kernel, shape(count, cells), [swap, local, one, two])
    rank = lax.axis_index("orb").astype(jnp.int32)
    everyone = members == orb and orb & (orb - 1) == 0
    blocks = gather_all(work, orb) if everyone else gather_leading(work, rank, members)
    gram, stack = call(
        functools.partial(gram_kernel, scale),
        (shape(total, total), shape(2 * total, cells, dtype=jnp.bfloat16)),
        [rank.reshape(1) if everyone else jnp.zeros((1,), jnp.int32), *blocks],
    )
    parts = grid_sum(gram, grid)
    if not everyone:
        rest = finish_leading(work, blocks, sum(parts), rank, scale)
        return rest.reshape(count, depth, plane)
    done = call(
        finish_kernel,
        shape(depth, count, plane),
        [rank.reshape(1), *parts, stack],
        scratch=[pltpu.VMEM((total, total), jnp.float32)],
    )
    return jnp.transpose(done, (1, 0, 2))


def solution(mesh):
    return jax.shard_map(
        per_device,
        mesh=mesh,
        in_specs=(P("orb", "grid", None), P("grid", None)),
        out_specs=P("orb", "grid", None),
        check_vma=False,
    )
```

```python
import functools

import jax
import jax.numpy as jnp
from jax import lax
from jax.experimental import pallas as pl
from jax.experimental.pallas import tpu as pltpu
from jax.sharding import PartitionSpec as P

PANEL = 32
NPANEL = 2
NY = 32

COEFFS = (
    -5369.0 / 1800.0,
    12.0 / 7.0,
    -15.0 / 56.0,
    10.0 / 189.0,
    -1.0 / 112.0,
    2.0 / 1925.0,
    -1.0 / 16632.0,
)
HIGH = lax.Precision.HIGHEST
RIM = 6
LAST = 6
BOTH = ("orb", "grid")


def local_kernel(v_ref, pot_ref, out_ref):
    depth, count, plane = v_ref.shape
    lane = lax.broadcasted_iota(jnp.int32, (count, plane), 1)
    column = lane % NY
    for p in range(depth):
        here = v_ref[p]
        acc = (-1.5 * COEFFS[0] + pot_ref[p : p + 1, :]) * here
        for k in range(1, RIM + 1):
            up, down = NY * k, plane - NY * k
            near = jnp.where(lane < down, pltpu.roll(here, down, 1), 0.0)
            near += jnp.where(lane >= up, pltpu.roll(here, up, 1), 0.0)
            near += jnp.where(column + k < NY, pltpu.roll(here, plane - k, 1), 0.0)
            near += jnp.where(column >= k, pltpu.roll(here, k, 1), 0.0)
            if p + k < depth:
                near += v_ref[p + k]
            if p >= k:
                near += v_ref[p - k]
            acc += (-0.5 * COEFFS[k]) * near
        out_ref[:, p * plane : (p + 1) * plane] = acc


def couple_kernel(swap_ref, local_ref, one_ref, two_ref, out_ref):
    @pl.when(swap_ref[0] == 0)
    def _():
        couple(local_ref, one_ref, two_ref, out_ref)

    @pl.when(swap_ref[0] == 1)
    def _():
        couple(local_ref, two_ref, one_ref, out_ref)


def couple(local_ref, before_ref, after_ref, out_ref):
    rim, count, plane = before_ref.shape
    depth = out_ref.shape[1] // plane
    for p in range(depth):
        acc = local_ref[:, p * plane : (p + 1) * plane]
        for q in range(rim):
            if p + rim - q <= rim:
                acc += (-0.5 * COEFFS[p + rim - q]) * before_ref[q]
            if depth + q - p <= rim:
                acc += (-0.5 * COEFFS[depth + q - p]) * after_ref[q]
        out_ref[:, p * plane : (p + 1) * plane] = acc


def place(rank, mask, rows):
    return pl.multiple_of((rank // 2 ^ mask // 2) * rows, rows)


def store_pair(rank, mask, one_ref, two_ref, stack_ref):
    odd = rank % 2 == 1
    one, two = one_ref[...], two_ref[...]
    pair = jnp.concatenate([jnp.where(odd, two, one), jnp.where(odd, one, two)], 0)
    high = pair.astype(jnp.bfloat16)
    low = (pair - high.astype(jnp.float32)).astype(jnp.bfloat16)
    rows, half = pair.shape[0], stack_ref.shape[0] // 2
    first = place(rank, mask, rows)
    stack_ref[pl.ds(first, rows), :] = high
    stack_ref[pl.ds(half + first, rows), :] = low
    return jnp.concatenate([high, low], 0)


def products(left, right, scale):
    every = lax.dot_general(
        left, right, (((1,), (1,)), ((), ())), preferred_element_type=jnp.float32
    )
    rows, columns = left.shape[0] // 2, right.shape[0] // 2
    both = every[:rows] + every[rows:]
    return (both[:, :columns] + both[:, columns:]) * scale


def gram_kernel(scale, masks, rank_ref, *refs):
    blocks, (gram_ref, stack_ref) = refs[:-2], refs[-2:]
    rows = 2 * blocks[0].shape[0]
    half = stack_ref.shape[0] // 2
    rank = rank_ref[0]
    missing = place(rank, LAST, rows)
    blank = jnp.zeros((rows, stack_ref.shape[1]), jnp.bfloat16)
    stack_ref[pl.ds(missing, rows), :] = blank
    stack_ref[pl.ds(half + missing, rows), :] = blank
    for k, mask in enumerate(masks):
        store_pair(rank, mask, blocks[2 * k], blocks[2 * k + 1], stack_ref)
    whole = stack_ref[...]
    gram_ref[...] = products(whole, whole, scale)


def last_kernel(scale, rank_ref, one_ref, two_ref, early_ref, before_ref, gram_ref, stack_ref):
    rank = rank_ref[0]
    rows = 2 * one_ref.shape[0]
    total = gram_ref.shape[0]
    pair = store_pair(rank, LAST, one_ref, two_ref, stack_ref)
    lines = products(pair, stack_ref[...], scale)
    repeated = jnp.concatenate([lines] * (total // rows), 0)
    first = place(rank, LAST, rows)
    row = lax.broadcasted_iota(jnp.int32, (total, total), 0)
    column = lax.broadcasted_iota(jnp.int32, (total, total), 1)
    gram = jnp.where(
        (column >= first) & (column < first + rows), repeated.T, early_ref[...]
    )
    gram_ref[...] = jnp.where((row >= first) & (row < first + rows), repeated, gram)


def invert_factor(gram):
    size = gram.shape[0]
    rows = 8
    full = (rows, 2 * size)
    ident = (
        lax.broadcasted_iota(jnp.int32, (size, size), 0)
        == lax.broadcasted_iota(jnp.int32, (size, size), 1)
    ).astype(jnp.float32)
    zero = lax.broadcasted_iota(jnp.int32, full, 1).astype(jnp.float32) * 0.0
    whole = jnp.concatenate([gram, ident], 1)
    tiles = [whole[i : i + rows] for i in range(0, size, rows)]
    done = []
    for t in range(len(tiles)):

        def columns(i):
            first = t * rows
            return [
                jnp.broadcast_to(tiles[i][:, first + a : first + a + 1], full) for a in range(rows)
            ]

        own = [column + zero for column in columns(t)]
        after = columns(t + 1) if t + 1 < len(tiles) else None
        line = [jnp.broadcast_to(tiles[t][a : a + 1], full) for a in range(rows)]
        pivot = [
            [jnp.broadcast_to(own[b][a : a + 1], full) for b in range(a + 1)] for a in range(rows)
        ]
        factor = [[None] * rows for _ in range(rows)]
        scaled = []
        for a in range(rows):
            inverse = 1.0 / pivot[a][a]
            scaled.append(line[a] * inverse)
            for b in range(a + 1, rows):
                factor[b][a] = pivot[b][a] * inverse
                line[b] = line[b] - factor[b][a] * line[a]
                for c in range(a + 1, b + 1):
                    pivot[b][c] = pivot[b][c] - factor[b][a] * pivot[c][a]
            if after is not None:
                tiles[t + 1] = tiles[t + 1] - after[a] * scaled[a]
                for b in range(a + 1, rows):
                    after[b] = after[b] - factor[b][a] * after[a]
        done += [(line[a] * lax.rsqrt(pivot[a][a]))[:1] for a in range(rows)]
        for a in range(rows - 1, -1, -1):
            for b in range(a):
                scaled[b] = scaled[b] - factor[a][b] * scaled[a]
        for i in range(t + 2, len(tiles)):
            terms = [column * scaled[a] for a, column in enumerate(columns(i))]
            while len(terms) > 1:
                terms = [terms[k] + terms[k + 1] for k in range(0, len(terms), 2)]
            tiles[i] = tiles[i] - terms[0]
    return jnp.concatenate(done, 0)[:, size:]


def finish_kernel(rank_ref, *refs):
    parts, (stack_ref, out_ref, factor_ref) = refs[:-3], refs[-3:]
    depth, count, plane = out_ref.shape
    gram = parts[0][...]
    for part in parts[1:]:
        gram = gram + part[...]
    factor_ref[...] = invert_factor(gram)
    rows = factor_ref[pl.ds(pl.multiple_of(rank_ref[0] * count, count), count), :]
    high = rows.astype(jnp.bfloat16).astype(jnp.float32)
    low = rows - high
    left = jnp.concatenate(
        [jnp.concatenate([high, high], 1), jnp.concatenate([low, low], 1)], 0
    ).astype(jnp.bfloat16)
    for p in range(depth):
        both = jnp.dot(
            left, stack_ref[:, p * plane : (p + 1) * plane], preferred_element_type=jnp.float32
        )
        out_ref[p] = both[:count] + both[count:]


def call(kernel, out_shape, inputs, scratch=(), flops=0, aliases=None):
    in_specs = [
        pl.BlockSpec(memory_space=pltpu.SMEM if a.dtype == jnp.int32 else pltpu.VMEM)
        for a in inputs
    ]
    out_specs = jax.tree.map(lambda s: pl.BlockSpec(memory_space=pltpu.VMEM), out_shape)
    return pl.pallas_call(
        kernel,
        out_shape=out_shape,
        in_specs=in_specs,
        out_specs=out_specs,
        scratch_shapes=scratch,
        input_output_aliases=aliases or {},
        compiler_params=pltpu.CompilerParams(vmem_limit_bytes=32 * 2**20),
        cost_estimate=pl.CostEstimate(flops=flops, bytes_accessed=10**6, transcendentals=0),
    )(*inputs)


def rotation(peers, step):
    return [(i, (i + step) % peers) for i in range(peers)]


def partners(orb, grid, masks, core=0):
    return [
        (o * grid + g, (o ^ core) * grid + (g ^ masks[o % 2]))
        for o in range(orb)
        for g in range(grid)
    ]


def exchange(peers, mask):
    return [(i, i ^ mask) for i in range(peers)]


def shape(*dims, dtype=jnp.float32):
    return jax.ShapeDtypeStruct(dims, dtype)


def halo(planes, orb, grid):
    depth = planes.shape[0]
    if grid == 4 and depth == RIM:
        one = lax.ppermute(planes, BOTH, partners(orb, grid, (3, 1)))
        two = lax.ppermute(planes, BOTH, partners(orb, grid, (1, 3)))
        swap = (lax.axis_index("grid") + lax.axis_index("orb")) % 2
        return one, two, swap.astype(jnp.int32).reshape(1)
    before = lax.ppermute(planes[depth - RIM :], "grid", rotation(grid, 1))
    after = lax.ppermute(planes[:RIM], "grid", rotation(grid, -1))
    return before, after, jnp.zeros((1,), jnp.int32)


def grid_sum(part, orb, grid):
    if grid != 4:
        return [lax.psum(part, "grid")]
    sets = [partners(orb, grid, (k, k), 1) for k in (2, 1, 3)]
    return [part] + [lax.ppermute(part, BOTH, pairs) for pairs in sets]


def gather_all(work, orb, scale, rank):
    count, cells = work.shape
    total = orb * count
    pairs = []
    masks = (0, 2, 4, LAST)
    for mask in masks:
        block = work if mask == 0 else lax.ppermute(work, "orb", exchange(orb, mask))
        pairs.append([block, lax.ppermute(block, "orb", exchange(orb, 1))])
    outs = (shape(total, total), shape(2 * total, cells, dtype=jnp.bfloat16))
    early, before = call(
        functools.partial(gram_kernel, scale, masks[:-1]), outs, [rank, *sum(pairs[:-1], [])]
    )
    return call(
        functools.partial(last_kernel, scale),
        outs,
        [rank, *pairs[-1], early, before],
        aliases={4: 1},
    )


def gather_leading(work, rank, members):
    kept = [jnp.where(rank == m, work, jnp.zeros_like(work)) for m in range(members)]
    return lax.psum(kept, "orb")


def finish_leading(work, blocks, gram, rank, scale):
    count = work.shape[0]
    leading = jnp.concatenate(blocks, 0)
    total = leading.shape[0]
    inner = functools.partial(jnp.einsum, "ic,jc->ij", precision=HIGH)
    coeff = lax.psum(inner(work, leading) * scale, "grid")
    inverse = lax.linalg.triangular_solve(
        jnp.linalg.cholesky(gram), jnp.eye(total, dtype=gram.dtype), left_side=True, lower=True
    )
    first = jnp.minimum(rank * count, total - count)
    owned = lax.dynamic_slice_in_dim(inverse, first, count, 0)
    taken = jnp.dot(inner(coeff, inverse), inverse, precision=HIGH)
    member = rank * count < total
    rows = jnp.where(member, owned, -taken)
    return jnp.where(member, 0.0, work) + jnp.dot(rows, leading, precision=HIGH)


def per_device(wavefunctions, potential):
    planes = jnp.transpose(wavefunctions, (1, 0, 2))
    depth, count, plane = planes.shape
    cells = depth * plane
    orb, grid = lax.axis_size("orb"), lax.axis_size("grid")
    members = min(PANEL * NPANEL // count, orb)
    total = members * count
    scale = 1.0 / (cells * grid)
    one, two, swap = halo(planes, orb, grid)
    local = call(local_kernel, shape(count, cells), [planes, potential], flops=10**9)
    work = call(couple_kernel, shape(count, cells), [swap, local, one, two])
    rank = lax.axis_index("orb").astype(jnp.int32)
    everyone = members == orb == 8
    if everyone:
        gram, stack = gather_all(work, orb, scale, rank.reshape(1))
    else:
        blocks = gather_leading(work, rank, members)
        leading = jnp.concatenate(blocks, 0)
        gram = jnp.einsum("ic,jc->ij", leading, leading, precision=HIGH) * scale
    parts = grid_sum(gram, orb, grid)
    if not everyone:
        rest = finish_leading(work, blocks, sum(parts), rank, scale)
        return rest.reshape(count, depth, plane)
    done = call(
        finish_kernel,
        shape(depth, count, plane),
        [rank.reshape(1), *parts, stack],
        scratch=[pltpu.VMEM((total, total), jnp.float32)],
    )
    return jnp.transpose(done, (1, 0, 2))


def solution(mesh):
    return jax.shard_map(
        per_device,
        mesh=mesh,
        in_specs=(P("orb", "grid", None), P("grid", None)),
        out_specs=P("orb", "grid", None),
        check_vma=False,
    )
```

```python
import functools

import jax
import jax.numpy as jnp
from jax import lax
from jax.experimental import pallas as pl
from jax.experimental.pallas import tpu as pltpu
from jax.sharding import PartitionSpec as P

PANEL = 32
NPANEL = 2
NY = 32

COEFFS = (
    -5369.0 / 1800.0,
    12.0 / 7.0,
    -15.0 / 56.0,
    10.0 / 189.0,
    -1.0 / 112.0,
    2.0 / 1925.0,
    -1.0 / 16632.0,
)
HIGH = lax.Precision.HIGHEST
RIM = 6
LAST = 6
BOTH = ("orb", "grid")


def local_kernel(v_ref, pot_ref, out_ref):
    depth, count, plane = v_ref.shape
    lane = lax.broadcasted_iota(jnp.int32, (count, plane), 1)
    column = lane % NY
    for p in range(depth):
        here = v_ref[p]
        acc = (-1.5 * COEFFS[0] + pot_ref[p : p + 1, :]) * here
        for k in range(1, RIM + 1):
            up, down = NY * k, plane - NY * k
            near = jnp.where(lane < down, pltpu.roll(here, down, 1), 0.0)
            near += jnp.where(lane >= up, pltpu.roll(here, up, 1), 0.0)
            near += jnp.where(column + k < NY, pltpu.roll(here, plane - k, 1), 0.0)
            near += jnp.where(column >= k, pltpu.roll(here, k, 1), 0.0)
            if p + k < depth:
                near += v_ref[p + k]
            if p >= k:
                near += v_ref[p - k]
            acc += (-0.5 * COEFFS[k]) * near
        out_ref[:, p * plane : (p + 1) * plane] = acc


def couple_kernel(swap_ref, local_ref, one_ref, two_ref, out_ref):
    @pl.when(swap_ref[0] == 0)
    def _():
        couple(local_ref, one_ref, two_ref, out_ref)

    @pl.when(swap_ref[0] == 1)
    def _():
        couple(local_ref, two_ref, one_ref, out_ref)


def couple(local_ref, before_ref, after_ref, out_ref):
    rim, count, plane = before_ref.shape
    depth = out_ref.shape[1] // plane
    for p in range(depth):
        acc = local_ref[:, p * plane : (p + 1) * plane]
        for q in range(rim):
            if p + rim - q <= rim:
                acc += (-0.5 * COEFFS[p + rim - q]) * before_ref[q]
            if depth + q - p <= rim:
                acc += (-0.5 * COEFFS[depth + q - p]) * after_ref[q]
        out_ref[:, p * plane : (p + 1) * plane] = acc


def place(rank, mask, rows):
    return pl.multiple_of((rank // 2 ^ mask // 2) * rows, rows)


def store_pair(rank, mask, one_ref, two_ref, stack_ref):
    odd = rank % 2 == 1
    one, two = one_ref[...], two_ref[...]
    pair = jnp.concatenate([jnp.where(odd, two, one), jnp.where(odd, one, two)], 0)
    high = pair.astype(jnp.bfloat16)
    low = (pair - high.astype(jnp.float32)).astype(jnp.bfloat16)
    rows, half = pair.shape[0], stack_ref.shape[0] // 2
    first = place(rank, mask, rows)
    stack_ref[pl.ds(first, rows), :] = high
    stack_ref[pl.ds(half + first, rows), :] = low
    return jnp.concatenate([high, low], 0)


def products(left, right, scale):
    every = lax.dot_general(
        left, right, (((1,), (1,)), ((), ())), preferred_element_type=jnp.float32
    )
    rows, columns = left.shape[0] // 2, right.shape[0] // 2
    both = every[:rows] + every[rows:]
    return (both[:, :columns] + both[:, columns:]) * scale


def gram_kernel(scale, masks, rank_ref, *refs):
    blocks, (gram_ref, stack_ref) = refs[:-2], refs[-2:]
    rows = 2 * blocks[0].shape[0]
    half = stack_ref.shape[0] // 2
    rank = rank_ref[0]
    missing = place(rank, LAST, rows)
    blank = jnp.zeros((rows, stack_ref.shape[1]), jnp.bfloat16)
    stack_ref[pl.ds(missing, rows), :] = blank
    stack_ref[pl.ds(half + missing, rows), :] = blank
    for k, mask in enumerate(masks):
        store_pair(rank, mask, blocks[2 * k], blocks[2 * k + 1], stack_ref)
    whole = stack_ref[...]
    gram_ref[...] = products(whole, whole, scale)


def last_kernel(scale, rank_ref, one_ref, two_ref, early_ref, before_ref, gram_ref, stack_ref):
    rank = rank_ref[0]
    rows = 2 * one_ref.shape[0]
    total = gram_ref.shape[0]
    pair = store_pair(rank, LAST, one_ref, two_ref, stack_ref)
    lines = products(pair, stack_ref[...], scale)
    repeated = jnp.concatenate([lines] * (total // rows), 0)
    first = place(rank, LAST, rows)
    row = lax.broadcasted_iota(jnp.int32, (total, total), 0)
    column = lax.broadcasted_iota(jnp.int32, (total, total), 1)
    gram = jnp.where(
        (column >= first) & (column < first + rows), repeated.T, early_ref[...]
    )
    gram_ref[...] = jnp.where((row >= first) & (row < first + rows), repeated, gram)


def invert_factor(gram):
    size = gram.shape[0]
    rows = 8
    full = (rows, 2 * size)
    ident = (
        lax.broadcasted_iota(jnp.int32, (size, size), 0)
        == lax.broadcasted_iota(jnp.int32, (size, size), 1)
    ).astype(jnp.float32)
    zero = lax.broadcasted_iota(jnp.int32, full, 1).astype(jnp.float32) * 0.0
    whole = jnp.concatenate([gram, ident], 1)
    tiles = [whole[i : i + rows] for i in range(0, size, rows)]

    def columns(i, first):
        return [jnp.broadcast_to(tiles[i][:, k : k + 1], full) for k in range(first, first + rows)]

    def spread(value, a):
        return jnp.broadcast_to(value[a : a + 1], full)

    own = [column + zero for column in columns(0, 0)]
    done = []
    for t in range(len(tiles)):
        last = t + 1 == len(tiles)
        if not last:
            after = [column + zero for column in columns(t + 1, t * rows)]
            following = [column + zero for column in columns(t + 1, (t + 1) * rows)]
        line = [spread(tiles[t], a) for a in range(rows)]
        pivot = [[spread(own[b], a) for b in range(a + 1)] for a in range(rows)]
        factor = [[None] * rows for _ in range(rows)]
        inverse = []
        for a in range(rows):
            inverse.append(1.0 / pivot[a][a])
            for b in range(a + 1, rows):
                factor[b][a] = pivot[b][a] * inverse[a]
                line[b] = line[b] - factor[b][a] * line[a]
                for c in range(a + 1, b + 1):
                    pivot[b][c] = pivot[b][c] - factor[b][a] * pivot[c][a]
        done += [(line[a] * lax.rsqrt(pivot[a][a]))[:1] for a in range(rows)]
        if last:
            break
        scaled = [line[a] * inverse[a] for a in range(rows)]
        for a in range(rows):
            tiles[t + 1] = tiles[t + 1] - after[a] * scaled[a]
            weight = after[a] * inverse[a]
            following = [f - weight * spread(after[a], c) for c, f in enumerate(following)]
            for b in range(a + 1, rows):
                after[b] = after[b] - factor[b][a] * after[a]
        for a in range(rows - 1, -1, -1):
            for b in range(a):
                scaled[b] = scaled[b] - factor[a][b] * scaled[a]
        for i in range(t + 2, len(tiles)):
            terms = [column * scaled[a] for a, column in enumerate(columns(i, t * rows))]
            while len(terms) > 1:
                terms = [terms[k] + terms[k + 1] for k in range(0, len(terms), 2)]
            tiles[i] = tiles[i] - terms[0]
        own = following
    return jnp.concatenate(done, 0)[:, size:]


def finish_kernel(rank_ref, *refs):
    parts, (stack_ref, out_ref, factor_ref) = refs[:-3], refs[-3:]
    depth, count, plane = out_ref.shape
    gram = parts[0][...]
    for part in parts[1:]:
        gram = gram + part[...]
    factor_ref[...] = invert_factor(gram)
    rows = factor_ref[pl.ds(pl.multiple_of(rank_ref[0] * count, count), count), :]
    high = rows.astype(jnp.bfloat16).astype(jnp.float32)
    low = rows - high
    left = jnp.concatenate(
        [jnp.concatenate([high, high], 1), jnp.concatenate([low, low], 1)], 0
    ).astype(jnp.bfloat16)
    for p in range(depth):
        both = jnp.dot(
            left, stack_ref[:, p * plane : (p + 1) * plane], preferred_element_type=jnp.float32
        )
        out_ref[p] = both[:count] + both[count:]


def call(kernel, out_shape, inputs, scratch=(), flops=0, aliases=None):
    in_specs = [
        pl.BlockSpec(memory_space=pltpu.SMEM if a.dtype == jnp.int32 else pltpu.VMEM)
        for a in inputs
    ]
    out_specs = jax.tree.map(lambda s: pl.BlockSpec(memory_space=pltpu.VMEM), out_shape)
    return pl.pallas_call(
        kernel,
        out_shape=out_shape,
        in_specs=in_specs,
        out_specs=out_specs,
        scratch_shapes=scratch,
        input_output_aliases=aliases or {},
        compiler_params=pltpu.CompilerParams(vmem_limit_bytes=32 * 2**20),
        cost_estimate=pl.CostEstimate(flops=flops, bytes_accessed=10**6, transcendentals=0),
    )(*inputs)


def rotation(peers, step):
    return [(i, (i + step) % peers) for i in range(peers)]


def partners(orb, grid, masks, core=0):
    return [
        (o * grid + g, (o ^ core) * grid + (g ^ masks[o % 2]))
        for o in range(orb)
        for g in range(grid)
    ]


def exchange(peers, mask):
    return [(i, i ^ mask) for i in range(peers)]


def shape(*dims, dtype=jnp.float32):
    return jax.ShapeDtypeStruct(dims, dtype)


def halo(planes, orb, grid):
    depth = planes.shape[0]
    if grid == 4 and depth == RIM:
        one = lax.ppermute(planes, BOTH, partners(orb, grid, (3, 1)))
        two = lax.ppermute(planes, BOTH, partners(orb, grid, (1, 3)))
        swap = (lax.axis_index("grid") + lax.axis_index("orb")) % 2
        return one, two, swap.astype(jnp.int32).reshape(1)
    before = lax.ppermute(planes[depth - RIM :], "grid", rotation(grid, 1))
    after = lax.ppermute(planes[:RIM], "grid", rotation(grid, -1))
    return before, after, jnp.zeros((1,), jnp.int32)


def grid_sum(part, orb, grid):
    if grid != 4:
        return [lax.psum(part, "grid")]
    sets = [partners(orb, grid, (k, k), 1) for k in (2, 1, 3)]
    return [part] + [lax.ppermute(part, BOTH, pairs) for pairs in sets]


def gather_all(work, orb, scale, rank):
    count, cells = work.shape
    total = orb * count
    pairs = []
    masks = (0, 2, 4, LAST)
    for mask in masks:
        block = work if mask == 0 else lax.ppermute(work, "orb", exchange(orb, mask))
        pairs.append([block, lax.ppermute(block, "orb", exchange(orb, 1))])
    outs = (shape(total, total), shape(2 * total, cells, dtype=jnp.bfloat16))
    early, before = call(
        functools.partial(gram_kernel, scale, masks[:-1]), outs, [rank, *sum(pairs[:-1], [])]
    )
    return call(
        functools.partial(last_kernel, scale),
        outs,
        [rank, *pairs[-1], early, before],
        aliases={4: 1},
    )


def gather_leading(work, rank, members):
    kept = [jnp.where(rank == m, work, jnp.zeros_like(work)) for m in range(members)]
    return lax.psum(kept, "orb")


def finish_leading(work, blocks, gram, rank, scale):
    count = work.shape[0]
    leading = jnp.concatenate(blocks, 0)
    total = leading.shape[0]
    inner = functools.partial(jnp.einsum, "ic,jc->ij", precision=HIGH)
    coeff = lax.psum(inner(work, leading) * scale, "grid")
    inverse = lax.linalg.triangular_solve(
        jnp.linalg.cholesky(gram), jnp.eye(total, dtype=gram.dtype), left_side=True, lower=True
    )
    first = jnp.minimum(rank * count, total - count)
    owned = lax.dynamic_slice_in_dim(inverse, first, count, 0)
    taken = jnp.dot(inner(coeff, inverse), inverse, precision=HIGH)
    member = rank * count < total
    rows = jnp.where(member, owned, -taken)
    return jnp.where(member, 0.0, work) + jnp.dot(rows, leading, precision=HIGH)


def per_device(wavefunctions, potential):
    planes = jnp.transpose(wavefunctions, (1, 0, 2))
    depth, count, plane = planes.shape
    cells = depth * plane
    orb, grid = lax.axis_size("orb"), lax.axis_size("grid")
    members = min(PANEL * NPANEL // count, orb)
    total = members * count
    scale = 1.0 / (cells * grid)
    one, two, swap = halo(planes, orb, grid)
    local = call(local_kernel, shape(count, cells), [planes, potential], flops=10**9)
    work = call(couple_kernel, shape(count, cells), [swap, local, one, two])
    rank = lax.axis_index("orb").astype(jnp.int32)
    everyone = members == orb == 8
    if everyone:
        gram, stack = gather_all(work, orb, scale, rank.reshape(1))
    else:
        blocks = gather_leading(work, rank, members)
        leading = jnp.concatenate(blocks, 0)
        gram = jnp.einsum("ic,jc->ij", leading, leading, precision=HIGH) * scale
    parts = grid_sum(gram, orb, grid)
    if not everyone:
        rest = finish_leading(work, blocks, sum(parts), rank, scale)
        return rest.reshape(count, depth, plane)
    done = call(
        finish_kernel,
        shape(depth, count, plane),
        [rank.reshape(1), *parts, stack],
        scratch=[pltpu.VMEM((total, total), jnp.float32)],
    )
    return jnp.transpose(done, (1, 0, 2))


def solution(mesh):
    return jax.shard_map(
        per_device,
        mesh=mesh,
        in_specs=(P("orb", "grid", None), P("grid", None)),
        out_specs=P("orb", "grid", None),
        check_vma=False,
    )
```

```python
import functools

import jax
import jax.numpy as jnp
from jax import lax
from jax.experimental import pallas as pl
from jax.experimental.pallas import tpu as pltpu
from jax.sharding import PartitionSpec as P

PANEL = 32
NPANEL = 2
NY = 32

COEFFS = (
    -5369.0 / 1800.0,
    12.0 / 7.0,
    -15.0 / 56.0,
    10.0 / 189.0,
    -1.0 / 112.0,
    2.0 / 1925.0,
    -1.0 / 16632.0,
)
HIGH = lax.Precision.HIGHEST
RIM = 6
LAST = 6
BOTH = ("orb", "grid")


def local_kernel(v_ref, pot_ref, out_ref):
    depth, count, plane = v_ref.shape
    lane = lax.broadcasted_iota(jnp.int32, (count, plane), 1)
    column = lane % NY
    for p in range(depth):
        here = v_ref[p]
        acc = (-1.5 * COEFFS[0] + pot_ref[p : p + 1, :]) * here
        for k in range(1, RIM + 1):
            up, down = NY * k, plane - NY * k
            near = jnp.where(lane < down, pltpu.roll(here, down, 1), 0.0)
            near += jnp.where(lane >= up, pltpu.roll(here, up, 1), 0.0)
            near += jnp.where(column + k < NY, pltpu.roll(here, plane - k, 1), 0.0)
            near += jnp.where(column >= k, pltpu.roll(here, k, 1), 0.0)
            if p + k < depth:
                near += v_ref[p + k]
            if p >= k:
                near += v_ref[p - k]
            acc += (-0.5 * COEFFS[k]) * near
        out_ref[:, p * plane : (p + 1) * plane] = acc


def couple_kernel(swap_ref, local_ref, one_ref, two_ref, out_ref):
    @pl.when(swap_ref[0] == 0)
    def _():
        couple(local_ref, one_ref, two_ref, out_ref)

    @pl.when(swap_ref[0] == 1)
    def _():
        couple(local_ref, two_ref, one_ref, out_ref)


def couple(local_ref, before_ref, after_ref, out_ref):
    rim, count, plane = before_ref.shape
    depth = out_ref.shape[1] // plane
    for p in range(depth):
        acc = local_ref[:, p * plane : (p + 1) * plane]
        for q in range(rim):
            if p + rim - q <= rim:
                acc += (-0.5 * COEFFS[p + rim - q]) * before_ref[q]
            if depth + q - p <= rim:
                acc += (-0.5 * COEFFS[depth + q - p]) * after_ref[q]
        out_ref[:, p * plane : (p + 1) * plane] = acc


def place(rank, mask, rows):
    return pl.multiple_of((rank // 2 ^ mask // 2) * rows, rows)


def store_pair(rank, mask, one_ref, two_ref, stack_ref):
    odd = rank % 2 == 1
    one, two = one_ref[...], two_ref[...]
    pair = jnp.concatenate([jnp.where(odd, two, one), jnp.where(odd, one, two)], 0)
    high = pair.astype(jnp.bfloat16)
    low = (pair - high.astype(jnp.float32)).astype(jnp.bfloat16)
    rows, half = pair.shape[0], stack_ref.shape[0] // 2
    first = place(rank, mask, rows)
    stack_ref[pl.ds(first, rows), :] = high
    stack_ref[pl.ds(half + first, rows), :] = low
    return jnp.concatenate([high, low], 0)


def products(left, right, scale):
    every = lax.dot_general(
        left, right, (((1,), (1,)), ((), ())), preferred_element_type=jnp.float32
    )
    rows, columns = left.shape[0] // 2, right.shape[0] // 2
    both = every[:rows] + every[rows:]
    return (both[:, :columns] + both[:, columns:]) * scale


def gram_kernel(scale, masks, rank_ref, *refs):
    blocks, (gram_ref, stack_ref) = refs[:-2], refs[-2:]
    rows = 2 * blocks[0].shape[0]
    half = stack_ref.shape[0] // 2
    rank = rank_ref[0]
    missing = place(rank, LAST, rows)
    blank = jnp.zeros((rows, stack_ref.shape[1]), jnp.bfloat16)
    stack_ref[pl.ds(missing, rows), :] = blank
    stack_ref[pl.ds(half + missing, rows), :] = blank
    for k, mask in enumerate(masks):
        store_pair(rank, mask, blocks[2 * k], blocks[2 * k + 1], stack_ref)
    whole = stack_ref[...]
    gram_ref[...] = products(whole, whole, scale)


def last_kernel(scale, rank_ref, one_ref, two_ref, early_ref, before_ref, gram_ref, stack_ref):
    rank = rank_ref[0]
    rows = 2 * one_ref.shape[0]
    total = gram_ref.shape[0]
    needed = (rank // 2 ^ LAST // 2) < rank // 2

    @pl.when(needed)
    def _():
        pair = store_pair(rank, LAST, one_ref, two_ref, stack_ref)
        lines = products(pair, stack_ref[...], scale)
        repeated = jnp.concatenate([lines] * (total // rows), 0)
        first = place(rank, LAST, rows)
        row = lax.broadcasted_iota(jnp.int32, (total, total), 0)
        column = lax.broadcasted_iota(jnp.int32, (total, total), 1)
        gram = jnp.where((column >= first) & (column < first + rows), repeated.T, early_ref[...])
        gram_ref[...] = jnp.where((row >= first) & (row < first + rows), repeated, gram)

    @pl.when(jnp.logical_not(needed))
    def _():
        gram_ref[...] = early_ref[...]


def invert_factor(gram, leading):
    size = gram.shape[0]
    rows = 8
    full = (rows, 2 * size)
    ident = (
        lax.broadcasted_iota(jnp.int32, (size, size), 0)
        == lax.broadcasted_iota(jnp.int32, (size, size), 1)
    ).astype(jnp.float32)
    zero = lax.broadcasted_iota(jnp.int32, full, 1).astype(jnp.float32) * 0.0
    whole = jnp.concatenate([gram, ident], 1)
    tiles = [whole[i : i + rows] for i in range(0, leading, rows)]

    def columns(i, first):
        return [jnp.broadcast_to(tiles[i][:, k : k + 1], full) for k in range(first, first + rows)]

    def spread(value, a):
        return jnp.broadcast_to(value[a : a + 1], full)

    own = [column + zero for column in columns(0, 0)]
    done = []
    for t in range(len(tiles)):
        last = t + 1 == len(tiles)
        if not last:
            after = [column + zero for column in columns(t + 1, t * rows)]
            following = [column + zero for column in columns(t + 1, (t + 1) * rows)]
        line = [spread(tiles[t], a) for a in range(rows)]
        pivot = [[spread(own[b], a) for b in range(a + 1)] for a in range(rows)]
        factor = [[None] * rows for _ in range(rows)]
        inverse = []
        for a in range(rows):
            inverse.append(1.0 / pivot[a][a])
            for b in range(a + 1, rows):
                factor[b][a] = pivot[b][a] * inverse[a]
                line[b] = line[b] - factor[b][a] * line[a]
                for c in range(a + 1, b + 1):
                    pivot[b][c] = pivot[b][c] - factor[b][a] * pivot[c][a]
        done += [(line[a] * lax.rsqrt(pivot[a][a]))[:1] for a in range(rows)]
        if last:
            break
        scaled = [line[a] * inverse[a] for a in range(rows)]
        for a in range(rows):
            tiles[t + 1] = tiles[t + 1] - after[a] * scaled[a]
            weight = after[a] * inverse[a]
            following = [f - weight * spread(after[a], c) for c, f in enumerate(following)]
            for b in range(a + 1, rows):
                after[b] = after[b] - factor[b][a] * after[a]
        for a in range(rows - 1, -1, -1):
            for b in range(a):
                scaled[b] = scaled[b] - factor[a][b] * scaled[a]
        for i in range(t + 2, len(tiles)):
            terms = [column * scaled[a] for a, column in enumerate(columns(i, t * rows))]
            while len(terms) > 1:
                terms = [terms[k] + terms[k + 1] for k in range(0, len(terms), 2)]
            tiles[i] = tiles[i] - terms[0]
        own = following
    return jnp.concatenate(done, 0)[:, size:]


def finish_kernel(rank_ref, *refs):
    parts, (stack_ref, out_ref, factor_ref) = refs[:-3], refs[-3:]
    depth, count, plane = out_ref.shape
    gram = parts[0][...]
    for part in parts[1:]:
        gram = gram + part[...]
    held = 2 * count
    chip = rank_ref[0] // 2
    low_chip = 0
    for top in (2, 4):

        @pl.when((chip >= low_chip) & (chip < top))
        def _(top=top):
            factor_ref[: top * held, :] = invert_factor(gram, top * held)

        low_chip = top
    rows = factor_ref[pl.ds(pl.multiple_of(rank_ref[0] * count, count), count), :]
    high = rows.astype(jnp.bfloat16).astype(jnp.float32)
    low = rows - high
    left = jnp.concatenate(
        [jnp.concatenate([high, high], 1), jnp.concatenate([low, low], 1)], 0
    ).astype(jnp.bfloat16)
    for p in range(depth):
        both = jnp.dot(
            left, stack_ref[:, p * plane : (p + 1) * plane], preferred_element_type=jnp.float32
        )
        out_ref[p] = both[:count] + both[count:]


def call(kernel, out_shape, inputs, scratch=(), flops=0, aliases=None):
    in_specs = [
        pl.BlockSpec(memory_space=pltpu.SMEM if a.dtype == jnp.int32 else pltpu.VMEM)
        for a in inputs
    ]
    out_specs = jax.tree.map(lambda s: pl.BlockSpec(memory_space=pltpu.VMEM), out_shape)
    return pl.pallas_call(
        kernel,
        out_shape=out_shape,
        in_specs=in_specs,
        out_specs=out_specs,
        scratch_shapes=scratch,
        input_output_aliases=aliases or {},
        compiler_params=pltpu.CompilerParams(vmem_limit_bytes=32 * 2**20),
        cost_estimate=pl.CostEstimate(flops=flops, bytes_accessed=10**6, transcendentals=0),
    )(*inputs)


def rotation(peers, step):
    return [(i, (i + step) % peers) for i in range(peers)]


def partners(orb, grid, masks, core=0):
    return [
        (o * grid + g, (o ^ core) * grid + (g ^ masks[o % 2]))
        for o in range(orb)
        for g in range(grid)
    ]


def exchange(peers, mask):
    return [(i, i ^ mask) for i in range(peers)]


def shape(*dims, dtype=jnp.float32):
    return jax.ShapeDtypeStruct(dims, dtype)


def halo(planes, orb, grid):
    depth = planes.shape[0]
    if grid == 4 and depth == RIM:
        one = lax.ppermute(planes, BOTH, partners(orb, grid, (3, 1)))
        two = lax.ppermute(planes, BOTH, partners(orb, grid, (1, 3)))
        swap = (lax.axis_index("grid") + lax.axis_index("orb")) % 2
        return one, two, swap.astype(jnp.int32).reshape(1)
    before = lax.ppermute(planes[depth - RIM :], "grid", rotation(grid, 1))
    after = lax.ppermute(planes[:RIM], "grid", rotation(grid, -1))
    return before, after, jnp.zeros((1,), jnp.int32)


def grid_sum(part, orb, grid):
    if grid != 4:
        return [lax.psum(part, "grid")]
    sets = [partners(orb, grid, (k, k), 1) for k in (2, 1, 3)]
    return [part] + [lax.ppermute(part, BOTH, pairs) for pairs in sets]


def gather_all(work, orb, scale, rank):
    count, cells = work.shape
    total = orb * count
    pairs = []
    masks = (0, 2, 4, LAST)
    for mask in masks:
        block = work if mask == 0 else lax.ppermute(work, "orb", exchange(orb, mask))
        pairs.append([block, lax.ppermute(block, "orb", exchange(orb, 1))])
    outs = (shape(total, total), shape(2 * total, cells, dtype=jnp.bfloat16))
    early, before = call(
        functools.partial(gram_kernel, scale, masks[:-1]), outs, [rank, *sum(pairs[:-1], [])]
    )
    return call(
        functools.partial(last_kernel, scale),
        outs,
        [rank, *pairs[-1], early, before],
        aliases={4: 1},
    )


def gather_leading(work, rank, members):
    kept = [jnp.where(rank == m, work, jnp.zeros_like(work)) for m in range(members)]
    return lax.psum(kept, "orb")


def finish_leading(work, blocks, gram, rank, scale):
    count = work.shape[0]
    leading = jnp.concatenate(blocks, 0)
    total = leading.shape[0]
    inner = functools.partial(jnp.einsum, "ic,jc->ij", precision=HIGH)
    coeff = lax.psum(inner(work, leading) * scale, "grid")
    inverse = lax.linalg.triangular_solve(
        jnp.linalg.cholesky(gram), jnp.eye(total, dtype=gram.dtype), left_side=True, lower=True
    )
    first = jnp.minimum(rank * count, total - count)
    owned = lax.dynamic_slice_in_dim(inverse, first, count, 0)
    taken = jnp.dot(inner(coeff, inverse), inverse, precision=HIGH)
    member = rank * count < total
    rows = jnp.where(member, owned, -taken)
    return jnp.where(member, 0.0, work) + jnp.dot(rows, leading, precision=HIGH)


def per_device(wavefunctions, potential):
    planes = jnp.transpose(wavefunctions, (1, 0, 2))
    depth, count, plane = planes.shape
    cells = depth * plane
    orb, grid = lax.axis_size("orb"), lax.axis_size("grid")
    members = min(PANEL * NPANEL // count, orb)
    total = members * count
    scale = 1.0 / (cells * grid)
    one, two, swap = halo(planes, orb, grid)
    local = call(local_kernel, shape(count, cells), [planes, potential], flops=10**9)
    work = call(couple_kernel, shape(count, cells), [swap, local, one, two])
    rank = lax.axis_index("orb").astype(jnp.int32)
    everyone = members == orb == 8
    if everyone:
        gram, stack = gather_all(work, orb, scale, rank.reshape(1))
    else:
        blocks = gather_leading(work, rank, members)
        leading = jnp.concatenate(blocks, 0)
        gram = jnp.einsum("ic,jc->ij", leading, leading, precision=HIGH) * scale
    parts = grid_sum(gram, orb, grid)
    if not everyone:
        rest = finish_leading(work, blocks, sum(parts), rank, scale)
        return rest.reshape(count, depth, plane)
    done = call(
        finish_kernel,
        shape(depth, count, plane),
        [rank.reshape(1), *parts, stack],
        scratch=[pltpu.VMEM((total, total), jnp.float32)],
    )
    return jnp.transpose(done, (1, 0, 2))


def solution(mesh):
    return jax.shard_map(
        per_device,
        mesh=mesh,
        in_specs=(P("orb", "grid", None), P("grid", None)),
        out_specs=P("orb", "grid", None),
        check_vma=False,
    )
```

```python
import functools

import jax
import jax.numpy as jnp
from jax import lax
from jax.experimental import pallas as pl
from jax.experimental.pallas import tpu as pltpu
from jax.sharding import PartitionSpec as P

PANEL = 32
NPANEL = 2
NY = 32

COEFFS = (
    -5369.0 / 1800.0,
    12.0 / 7.0,
    -15.0 / 56.0,
    10.0 / 189.0,
    -1.0 / 112.0,
    2.0 / 1925.0,
    -1.0 / 16632.0,
)
HIGH = lax.Precision.HIGHEST
RIM = 6
LAST = 6
BOTH = ("orb", "grid")


def local_kernel(v_ref, pot_ref, out_ref):
    depth, count, plane = v_ref.shape
    lane = lax.broadcasted_iota(jnp.int32, (count, plane), 1)
    column = lane % NY
    for p in range(depth):
        here = v_ref[p]
        acc = (-1.5 * COEFFS[0] + pot_ref[p : p + 1, :]) * here
        for k in range(1, RIM + 1):
            up, down = NY * k, plane - NY * k
            near = jnp.where(lane < down, pltpu.roll(here, down, 1), 0.0)
            near += jnp.where(lane >= up, pltpu.roll(here, up, 1), 0.0)
            near += jnp.where(column + k < NY, pltpu.roll(here, plane - k, 1), 0.0)
            near += jnp.where(column >= k, pltpu.roll(here, k, 1), 0.0)
            if p + k < depth:
                near += v_ref[p + k]
            if p >= k:
                near += v_ref[p - k]
            acc += (-0.5 * COEFFS[k]) * near
        out_ref[:, p * plane : (p + 1) * plane] = acc


def couple_kernel(swap_ref, local_ref, one_ref, two_ref, out_ref):
    @pl.when(swap_ref[0] == 0)
    def _():
        couple(local_ref, one_ref, two_ref, out_ref)

    @pl.when(swap_ref[0] == 1)
    def _():
        couple(local_ref, two_ref, one_ref, out_ref)


def couple(local_ref, before_ref, after_ref, out_ref):
    rim, count, plane = before_ref.shape
    depth = out_ref.shape[1] // plane
    for p in range(depth):
        acc = local_ref[:, p * plane : (p + 1) * plane]
        for q in range(rim):
            if p + rim - q <= rim:
                acc += (-0.5 * COEFFS[p + rim - q]) * before_ref[q]
            if depth + q - p <= rim:
                acc += (-0.5 * COEFFS[depth + q - p]) * after_ref[q]
        out_ref[:, p * plane : (p + 1) * plane] = acc


def place(rank, mask, rows):
    return pl.multiple_of((rank // 2 ^ mask // 2) * rows, rows)


def store_pair(rank, mask, one_ref, two_ref, stack_ref):
    odd = rank % 2 == 1
    one, two = one_ref[...], two_ref[...]
    pair = jnp.concatenate([jnp.where(odd, two, one), jnp.where(odd, one, two)], 0)
    high = pair.astype(jnp.bfloat16)
    low = (pair - high.astype(jnp.float32)).astype(jnp.bfloat16)
    rows, half = pair.shape[0], stack_ref.shape[0] // 2
    first = place(rank, mask, rows)
    stack_ref[pl.ds(first, rows), :] = high
    stack_ref[pl.ds(half + first, rows), :] = low
    return jnp.concatenate([high, low], 0)


def products(left, right, scale):
    every = lax.dot_general(
        left, right, (((1,), (1,)), ((), ())), preferred_element_type=jnp.float32
    )
    rows, columns = left.shape[0] // 2, right.shape[0] // 2
    both = every[:rows] + every[rows:]
    return (both[:, :columns] + both[:, columns:]) * scale


def gram_kernel(scale, masks, rank_ref, *refs):
    blocks, (gram_ref, stack_ref) = refs[:-2], refs[-2:]
    rows = 2 * blocks[0].shape[0]
    half = stack_ref.shape[0] // 2
    rank = rank_ref[0]
    missing = place(rank, LAST, rows)
    blank = jnp.zeros((rows, stack_ref.shape[1]), jnp.bfloat16)
    stack_ref[pl.ds(missing, rows), :] = blank
    stack_ref[pl.ds(half + missing, rows), :] = blank
    for k, mask in enumerate(masks):
        store_pair(rank, mask, blocks[2 * k], blocks[2 * k + 1], stack_ref)
    whole = stack_ref[...]
    gram_ref[...] = products(whole, whole, scale)


def last_kernel(scale, rank_ref, one_ref, two_ref, early_ref, before_ref, gram_ref, stack_ref):
    rank = rank_ref[0]
    rows = 2 * one_ref.shape[0]
    total = gram_ref.shape[0]
    needed = (rank // 2 ^ LAST // 2) < rank // 2

    @pl.when(needed)
    def _():
        pair = store_pair(rank, LAST, one_ref, two_ref, stack_ref)
        lines = products(pair, stack_ref[...], scale)
        repeated = jnp.concatenate([lines] * (total // rows), 0)
        first = place(rank, LAST, rows)
        row = lax.broadcasted_iota(jnp.int32, (total, total), 0)
        column = lax.broadcasted_iota(jnp.int32, (total, total), 1)
        gram = jnp.where((column >= first) & (column < first + rows), repeated.T, early_ref[...])
        gram_ref[...] = jnp.where((row >= first) & (row < first + rows), repeated, gram)

    @pl.when(jnp.logical_not(needed))
    def _():
        gram_ref[...] = early_ref[...]


def invert_factor(gram, leading):
    size = gram.shape[0]
    rows = 8
    full = (rows, 2 * size)
    ident = (
        lax.broadcasted_iota(jnp.int32, (size, size), 0)
        == lax.broadcasted_iota(jnp.int32, (size, size), 1)
    ).astype(jnp.float32)
    zero = lax.broadcasted_iota(jnp.int32, full, 1).astype(jnp.float32) * 0.0
    whole = jnp.concatenate([gram, ident], 1)
    tiles = [whole[i : i + rows] for i in range(0, leading, rows)]

    def columns(i, first):
        return [jnp.broadcast_to(tiles[i][:, k : k + 1], full) for k in range(first, first + rows)]

    def spread(value, a):
        return jnp.broadcast_to(value[a : a + 1], full)

    own = [column + zero for column in columns(0, 0)]
    done = []
    for t in range(len(tiles)):
        last = t + 1 == len(tiles)
        if not last:
            after = [column + zero for column in columns(t + 1, t * rows)]
            following = [column + zero for column in columns(t + 1, (t + 1) * rows)]
        line = [spread(tiles[t], a) for a in range(rows)]
        pivot = [[spread(own[b], a) for b in range(a + 1)] for a in range(rows)]
        factor = [[None] * rows for _ in range(rows)]
        inverse = []
        for a in range(rows):
            inverse.append(1.0 / pivot[a][a])
            for b in range(a + 1, rows):
                factor[b][a] = pivot[b][a] * inverse[a]
                line[b] = line[b] - factor[b][a] * line[a]
                for c in range(a + 1, b + 1):
                    pivot[b][c] = pivot[b][c] - factor[b][a] * pivot[c][a]
        done += [(line[a] * lax.rsqrt(pivot[a][a]))[:1] for a in range(rows)]
        if last:
            break
        scaled = [line[a] * inverse[a] for a in range(rows)]
        for a in range(rows):
            tiles[t + 1] = tiles[t + 1] - after[a] * scaled[a]
            weight = after[a] * inverse[a]
            following = [f - weight * spread(after[a], c) for c, f in enumerate(following)]
            for b in range(a + 1, rows):
                after[b] = after[b] - factor[b][a] * after[a]
        for a in range(rows - 1, -1, -1):
            for b in range(a):
                scaled[b] = scaled[b] - factor[a][b] * scaled[a]
        for i in range(t + 2, len(tiles)):
            terms = [column * scaled[a] for a, column in enumerate(columns(i, t * rows))]
            while len(terms) > 1:
                terms = [terms[k] + terms[k + 1] for k in range(0, len(terms), 2)]
            tiles[i] = tiles[i] - terms[0]
        own = following
    return jnp.concatenate(done, 0)[:, size:]


def finish_kernel(rank_ref, *refs):
    parts, (stack_ref, out_ref, factor_ref, held_ref, sems) = refs[:-5], refs[-5:]
    depth, count, plane = out_ref.shape
    gram = parts[0][...]
    for part in parts[1:]:
        gram = gram + part[...]
    held = 2 * count
    chip = rank_ref[0] // 2
    low_chip = 0
    for top in (2, 3, 4):

        @pl.when((chip >= low_chip) & (chip < top))
        def _(top=top):
            factor_ref[: top * held, :] = invert_factor(gram, top * held)

        low_chip = top
    rows = factor_ref[pl.ds(pl.multiple_of(rank_ref[0] * count, count), count), :]
    high = rows.astype(jnp.bfloat16).astype(jnp.float32)
    low = rows - high
    left = jnp.concatenate(
        [jnp.concatenate([high, high], 1), jnp.concatenate([low, low], 1)], 0
    ).astype(jnp.bfloat16)
    copies = []
    for p in range(depth):
        both = jnp.dot(
            left, stack_ref[:, p * plane : (p + 1) * plane], preferred_element_type=jnp.float32
        )
        held_ref[p] = both[:count] + both[count:]
        copies.append(pltpu.make_async_copy(held_ref.at[p], out_ref.at[p], sems.at[p]))
        copies[-1].start()
    for copy in copies:
        copy.wait()


def call(kernel, out_shape, inputs, scratch=(), flops=0, aliases=None, space=pltpu.VMEM):
    in_specs = [
        pl.BlockSpec(memory_space=pltpu.SMEM if a.dtype == jnp.int32 else pltpu.VMEM)
        for a in inputs
    ]
    out_specs = jax.tree.map(lambda s: pl.BlockSpec(memory_space=space), out_shape)
    return pl.pallas_call(
        kernel,
        out_shape=out_shape,
        in_specs=in_specs,
        out_specs=out_specs,
        scratch_shapes=scratch,
        input_output_aliases=aliases or {},
        compiler_params=pltpu.CompilerParams(vmem_limit_bytes=32 * 2**20),
        cost_estimate=pl.CostEstimate(flops=flops, bytes_accessed=10**6, transcendentals=0),
    )(*inputs)


def rotation(peers, step):
    return [(i, (i + step) % peers) for i in range(peers)]


def partners(orb, grid, masks, core=0):
    return [
        (o * grid + g, (o ^ core) * grid + (g ^ masks[o % 2]))
        for o in range(orb)
        for g in range(grid)
    ]


def exchange(peers, mask):
    return [(i, i ^ mask) for i in range(peers)]


def shape(*dims, dtype=jnp.float32):
    return jax.ShapeDtypeStruct(dims, dtype)


def halo(planes, orb, grid):
    depth = planes.shape[0]
    if grid == 4 and depth == RIM:
        one = lax.ppermute(planes, BOTH, partners(orb, grid, (3, 1)))
        two = lax.ppermute(planes, BOTH, partners(orb, grid, (1, 3)))
        swap = (lax.axis_index("grid") + lax.axis_index("orb")) % 2
        return one, two, swap.astype(jnp.int32).reshape(1)
    before = lax.ppermute(planes[depth - RIM :], "grid", rotation(grid, 1))
    after = lax.ppermute(planes[:RIM], "grid", rotation(grid, -1))
    return before, after, jnp.zeros((1,), jnp.int32)


def grid_sum(part, orb, grid):
    if grid != 4:
        return [lax.psum(part, "grid")]
    sets = [partners(orb, grid, (k, k), 1) for k in (2, 1, 3)]
    return [part] + [lax.ppermute(part, BOTH, pairs) for pairs in sets]


def gather_all(work, orb, scale, rank):
    count, cells = work.shape
    total = orb * count
    pairs = []
    masks = (0, 2, 4, LAST)
    for mask in masks:
        block = work if mask == 0 else lax.ppermute(work, "orb", exchange(orb, mask))
        pairs.append([block, lax.ppermute(block, "orb", exchange(orb, 1))])
    outs = (shape(total, total), shape(2 * total, cells, dtype=jnp.bfloat16))
    early, before = call(
        functools.partial(gram_kernel, scale, masks[:-1]), outs, [rank, *sum(pairs[:-1], [])]
    )
    return call(
        functools.partial(last_kernel, scale),
        outs,
        [rank, *pairs[-1], early, before],
        aliases={4: 1},
    )


def gather_leading(work, rank, members):
    kept = [jnp.where(rank == m, work, jnp.zeros_like(work)) for m in range(members)]
    return lax.psum(kept, "orb")


def finish_leading(work, blocks, gram, rank, scale):
    count = work.shape[0]
    leading = jnp.concatenate(blocks, 0)
    total = leading.shape[0]
    inner = functools.partial(jnp.einsum, "ic,jc->ij", precision=HIGH)
    coeff = lax.psum(inner(work, leading) * scale, "grid")
    inverse = lax.linalg.triangular_solve(
        jnp.linalg.cholesky(gram), jnp.eye(total, dtype=gram.dtype), left_side=True, lower=True
    )
    first = jnp.minimum(rank * count, total - count)
    owned = lax.dynamic_slice_in_dim(inverse, first, count, 0)
    taken = jnp.dot(inner(coeff, inverse), inverse, precision=HIGH)
    member = rank * count < total
    rows = jnp.where(member, owned, -taken)
    return jnp.where(member, 0.0, work) + jnp.dot(rows, leading, precision=HIGH)


def per_device(wavefunctions, potential):
    planes = jnp.transpose(wavefunctions, (1, 0, 2))
    depth, count, plane = planes.shape
    cells = depth * plane
    orb, grid = lax.axis_size("orb"), lax.axis_size("grid")
    members = min(PANEL * NPANEL // count, orb)
    total = members * count
    scale = 1.0 / (cells * grid)
    one, two, swap = halo(planes, orb, grid)
    local = call(local_kernel, shape(count, cells), [planes, potential], flops=10**9)
    work = call(couple_kernel, shape(count, cells), [swap, local, one, two])
    rank = lax.axis_index("orb").astype(jnp.int32)
    everyone = members == orb == 8
    if everyone:
        gram, stack = gather_all(work, orb, scale, rank.reshape(1))
    else:
        blocks = gather_leading(work, rank, members)
        leading = jnp.concatenate(blocks, 0)
        gram = jnp.einsum("ic,jc->ij", leading, leading, precision=HIGH) * scale
    parts = grid_sum(gram, orb, grid)
    if not everyone:
        rest = finish_leading(work, blocks, sum(parts), rank, scale)
        return rest.reshape(count, depth, plane)
    done = call(
        finish_kernel,
        shape(depth, count, plane),
        [rank.reshape(1), *parts, stack],
        scratch=[
            pltpu.VMEM((total, total), jnp.float32),
            pltpu.VMEM((depth, count, plane), jnp.float32),
            pltpu.SemaphoreType.DMA((depth,)),
        ],
        space=pl.ANY,
    )
    return jnp.transpose(done, (1, 0, 2))


def solution(mesh):
    return jax.shard_map(
        per_device,
        mesh=mesh,
        in_specs=(P("orb", "grid", None), P("grid", None)),
        out_specs=P("orb", "grid", None),
        check_vma=False,
    )
```

```python
import functools

import jax
import jax.numpy as jnp
from jax import lax
from jax.experimental import pallas as pl
from jax.experimental.pallas import tpu as pltpu
from jax.sharding import PartitionSpec as P

PANEL = 32
NPANEL = 2
NY = 32

COEFFS = (
    -5369.0 / 1800.0,
    12.0 / 7.0,
    -15.0 / 56.0,
    10.0 / 189.0,
    -1.0 / 112.0,
    2.0 / 1925.0,
    -1.0 / 16632.0,
)
HIGH = lax.Precision.HIGHEST
RIM = 6
LAST = 6
BOTH = ("orb", "grid")


def local_kernel(v_ref, pot_ref, out_ref):
    depth, count, plane = v_ref.shape
    lane = lax.broadcasted_iota(jnp.int32, (count, plane), 1)
    column = lane % NY
    for p in range(depth):
        here = v_ref[p]
        acc = (-1.5 * COEFFS[0] + pot_ref[p : p + 1, :]) * here
        for k in range(1, RIM + 1):
            up, down = NY * k, plane - NY * k
            near = jnp.where(lane < down, pltpu.roll(here, down, 1), 0.0)
            near += jnp.where(lane >= up, pltpu.roll(here, up, 1), 0.0)
            near += jnp.where(column + k < NY, pltpu.roll(here, plane - k, 1), 0.0)
            near += jnp.where(column >= k, pltpu.roll(here, k, 1), 0.0)
            if p + k < depth:
                near += v_ref[p + k]
            if p >= k:
                near += v_ref[p - k]
            acc += (-0.5 * COEFFS[k]) * near
        out_ref[:, p * plane : (p + 1) * plane] = acc


def couple_kernel(swap_ref, local_ref, one_ref, two_ref, out_ref):
    @pl.when(swap_ref[0] == 0)
    def _():
        couple(local_ref, one_ref, two_ref, out_ref)

    @pl.when(swap_ref[0] == 1)
    def _():
        couple(local_ref, two_ref, one_ref, out_ref)


def couple(local_ref, before_ref, after_ref, out_ref):
    rim, count, plane = before_ref.shape
    depth = out_ref.shape[1] // plane
    for p in range(depth):
        acc = local_ref[:, p * plane : (p + 1) * plane]
        for q in range(rim):
            if p + rim - q <= rim:
                acc += (-0.5 * COEFFS[p + rim - q]) * before_ref[q]
            if depth + q - p <= rim:
                acc += (-0.5 * COEFFS[depth + q - p]) * after_ref[q]
        out_ref[:, p * plane : (p + 1) * plane] = acc


def place(rank, mask, rows):
    return pl.multiple_of((rank // 2 ^ mask // 2) * rows, rows)


def store_pair(rank, mask, one_ref, two_ref, stack_ref):
    odd = rank % 2 == 1
    one, two = one_ref[...], two_ref[...]
    pair = jnp.concatenate([jnp.where(odd, two, one), jnp.where(odd, one, two)], 0)
    high = pair.astype(jnp.bfloat16)
    low = (pair - high.astype(jnp.float32)).astype(jnp.bfloat16)
    rows, half = pair.shape[0], stack_ref.shape[0] // 2
    first = place(rank, mask, rows)
    stack_ref[pl.ds(first, rows), :] = high
    stack_ref[pl.ds(half + first, rows), :] = low
    return jnp.concatenate([high, low], 0)


def products(left, right, scale):
    every = lax.dot_general(
        left, right, (((1,), (1,)), ((), ())), preferred_element_type=jnp.float32
    )
    rows, columns = left.shape[0] // 2, right.shape[0] // 2
    both = every[:rows] + every[rows:]
    return (both[:, :columns] + both[:, columns:]) * scale


def gram_kernel(scale, masks, rank_ref, *refs):
    blocks, (gram_ref, stack_ref) = refs[:-2], refs[-2:]
    rows = 2 * blocks[0].shape[0]
    half = stack_ref.shape[0] // 2
    rank = rank_ref[0]
    missing = place(rank, LAST, rows)
    blank = jnp.zeros((rows, stack_ref.shape[1]), jnp.bfloat16)
    stack_ref[pl.ds(missing, rows), :] = blank
    stack_ref[pl.ds(half + missing, rows), :] = blank
    for k, mask in enumerate(masks):
        store_pair(rank, mask, blocks[2 * k], blocks[2 * k + 1], stack_ref)
    whole = stack_ref[...]
    gram_ref[...] = products(whole, whole, scale)


def beside(gram):
    half = gram.shape[0] // 2
    return jnp.concatenate([gram[:half], gram[half:]], 1)


def last_kernel(scale, rank_ref, one_ref, two_ref, early_ref, before_ref, gram_ref, stack_ref):
    rank = rank_ref[0]
    rows = 2 * one_ref.shape[0]
    total = early_ref.shape[0]
    needed = (rank // 2 ^ LAST // 2) < rank // 2

    @pl.when(needed)
    def _():
        pair = store_pair(rank, LAST, one_ref, two_ref, stack_ref)
        lines = products(pair, stack_ref[...], scale)
        repeated = jnp.concatenate([lines] * (total // rows), 0)
        first = place(rank, LAST, rows)
        row = lax.broadcasted_iota(jnp.int32, (total, total), 0)
        column = lax.broadcasted_iota(jnp.int32, (total, total), 1)
        gram = jnp.where((column >= first) & (column < first + rows), repeated.T, early_ref[...])
        gram = jnp.where((row >= first) & (row < first + rows), repeated, gram)
        gram_ref[...] = beside(gram)

    @pl.when(jnp.logical_not(needed))
    def _():
        gram_ref[...] = beside(early_ref[...])


def invert_factor(gram, leading):
    size = gram.shape[0]
    rows = 8
    full = (rows, 2 * size)
    ident = (
        lax.broadcasted_iota(jnp.int32, (size, size), 0)
        == lax.broadcasted_iota(jnp.int32, (size, size), 1)
    ).astype(jnp.float32)
    zero = lax.broadcasted_iota(jnp.int32, full, 1).astype(jnp.float32) * 0.0
    whole = jnp.concatenate([gram, ident], 1)
    tiles = [whole[i : i + rows] for i in range(0, leading, rows)]

    def columns(i, first):
        return [jnp.broadcast_to(tiles[i][:, k : k + 1], full) for k in range(first, first + rows)]

    def spread(value, a):
        return jnp.broadcast_to(value[a : a + 1], full)

    own = [column + zero for column in columns(0, 0)]
    done = []
    for t in range(len(tiles)):
        last = t + 1 == len(tiles)
        if not last:
            after = [column + zero for column in columns(t + 1, t * rows)]
            following = [column + zero for column in columns(t + 1, (t + 1) * rows)]
        line = [spread(tiles[t], a) for a in range(rows)]
        pivot = [[spread(own[b], a) for b in range(a + 1)] for a in range(rows)]
        factor = [[None] * rows for _ in range(rows)]
        inverse = []
        for a in range(rows):
            inverse.append(1.0 / pivot[a][a])
            for b in range(a + 1, rows):
                factor[b][a] = pivot[b][a] * inverse[a]
                line[b] = line[b] - factor[b][a] * line[a]
                for c in range(a + 1, b + 1):
                    pivot[b][c] = pivot[b][c] - factor[b][a] * pivot[c][a]
        done += [(line[a] * lax.rsqrt(pivot[a][a]))[:1] for a in range(rows)]
        if last:
            break
        scaled = [line[a] * inverse[a] for a in range(rows)]
        for a in range(rows):
            tiles[t + 1] = tiles[t + 1] - after[a] * scaled[a]
            weight = after[a] * inverse[a]
            following = [f - weight * spread(after[a], c) for c, f in enumerate(following)]
            for b in range(a + 1, rows):
                after[b] = after[b] - factor[b][a] * after[a]
        for a in range(rows - 1, -1, -1):
            for b in range(a):
                scaled[b] = scaled[b] - factor[a][b] * scaled[a]
        for i in range(t + 2, len(tiles)):
            terms = [column * scaled[a] for a, column in enumerate(columns(i, t * rows))]
            while len(terms) > 1:
                terms = [terms[k] + terms[k + 1] for k in range(0, len(terms), 2)]
            tiles[i] = tiles[i] - terms[0]
        own = following
    return jnp.concatenate(done, 0)[:, size:]


def finish_kernel(rank_ref, *refs):
    parts, (stack_ref, out_ref, factor_ref) = refs[:-3], refs[-3:]
    depth, count, plane = out_ref.shape
    gram = parts[0][...]
    for part in parts[1:]:
        gram = gram + part[...]
    size = gram.shape[1] // 2
    gram = jnp.concatenate([gram[:, :size], gram[:, size:]], 0)
    held = 2 * count
    chip = rank_ref[0] // 2
    low_chip = 0
    for top in (2, 4):

        @pl.when((chip >= low_chip) & (chip < top))
        def _(top=top):
            factor_ref[: top * held, :] = invert_factor(gram, top * held)

        low_chip = top
    rows = factor_ref[pl.ds(pl.multiple_of(rank_ref[0] * count, count), count), :]
    high = rows.astype(jnp.bfloat16).astype(jnp.float32)
    low = rows - high
    left = jnp.concatenate(
        [jnp.concatenate([high, high], 1), jnp.concatenate([low, low], 1)], 0
    ).astype(jnp.bfloat16)
    for p in range(depth):
        both = jnp.dot(
            left, stack_ref[:, p * plane : (p + 1) * plane], preferred_element_type=jnp.float32
        )
        out_ref[p] = both[:count] + both[count:]


def call(kernel, out_shape, inputs, scratch=(), flops=0, aliases=None):
    in_specs = [
        pl.BlockSpec(memory_space=pltpu.SMEM if a.dtype == jnp.int32 else pltpu.VMEM)
        for a in inputs
    ]
    out_specs = jax.tree.map(lambda s: pl.BlockSpec(memory_space=pltpu.VMEM), out_shape)
    return pl.pallas_call(
        kernel,
        out_shape=out_shape,
        in_specs=in_specs,
        out_specs=out_specs,
        scratch_shapes=scratch,
        input_output_aliases=aliases or {},
        compiler_params=pltpu.CompilerParams(vmem_limit_bytes=32 * 2**20),
        cost_estimate=pl.CostEstimate(flops=flops, bytes_accessed=10**6, transcendentals=0),
    )(*inputs)


def rotation(peers, step):
    return [(i, (i + step) % peers) for i in range(peers)]


def partners(orb, grid, masks, core=0):
    return [
        (o * grid + g, (o ^ core) * grid + (g ^ masks[o % 2]))
        for o in range(orb)
        for g in range(grid)
    ]


def exchange(peers, mask):
    return [(i, i ^ mask) for i in range(peers)]


def shape(*dims, dtype=jnp.float32):
    return jax.ShapeDtypeStruct(dims, dtype)


def halo(planes, orb, grid):
    depth = planes.shape[0]
    if grid == 4 and depth == RIM:
        one = lax.ppermute(planes, BOTH, partners(orb, grid, (3, 1)))
        two = lax.ppermute(planes, BOTH, partners(orb, grid, (1, 3)))
        swap = (lax.axis_index("grid") + lax.axis_index("orb")) % 2
        return one, two, swap.astype(jnp.int32).reshape(1)
    before = lax.ppermute(planes[depth - RIM :], "grid", rotation(grid, 1))
    after = lax.ppermute(planes[:RIM], "grid", rotation(grid, -1))
    return before, after, jnp.zeros((1,), jnp.int32)


def grid_sum(part, orb, grid):
    if grid != 4:
        return [lax.psum(part, "grid")]
    sets = [partners(orb, grid, (k, k), 1) for k in (2, 1, 3)]
    return [part] + [lax.ppermute(part, BOTH, pairs) for pairs in sets]


def gather_all(work, orb, scale, rank):
    count, cells = work.shape
    total = orb * count
    pairs = []
    masks = (0, 2, 4, LAST)
    for mask in masks:
        block = work if mask == 0 else lax.ppermute(work, "orb", exchange(orb, mask))
        pairs.append([block, lax.ppermute(block, "orb", exchange(orb, 1))])
    outs = (shape(total, total), shape(2 * total, cells, dtype=jnp.bfloat16))
    early, before = call(
        functools.partial(gram_kernel, scale, masks[:-1]), outs, [rank, *sum(pairs[:-1], [])]
    )
    return call(
        functools.partial(last_kernel, scale),
        (shape(total // 2, 2 * total), outs[1]),
        [rank, *pairs[-1], early, before],
        aliases={4: 1},
    )


def gather_leading(work, rank, members):
    kept = [jnp.where(rank == m, work, jnp.zeros_like(work)) for m in range(members)]
    return lax.psum(kept, "orb")


def finish_leading(work, blocks, gram, rank, scale):
    count = work.shape[0]
    leading = jnp.concatenate(blocks, 0)
    total = leading.shape[0]
    inner = functools.partial(jnp.einsum, "ic,jc->ij", precision=HIGH)
    coeff = lax.psum(inner(work, leading) * scale, "grid")
    inverse = lax.linalg.triangular_solve(
        jnp.linalg.cholesky(gram), jnp.eye(total, dtype=gram.dtype), left_side=True, lower=True
    )
    first = jnp.minimum(rank * count, total - count)
    owned = lax.dynamic_slice_in_dim(inverse, first, count, 0)
    taken = jnp.dot(inner(coeff, inverse), inverse, precision=HIGH)
    member = rank * count < total
    rows = jnp.where(member, owned, -taken)
    return jnp.where(member, 0.0, work) + jnp.dot(rows, leading, precision=HIGH)


def per_device(wavefunctions, potential):
    planes = jnp.transpose(wavefunctions, (1, 0, 2))
    depth, count, plane = planes.shape
    cells = depth * plane
    orb, grid = lax.axis_size("orb"), lax.axis_size("grid")
    members = min(PANEL * NPANEL // count, orb)
    total = members * count
    scale = 1.0 / (cells * grid)
    one, two, swap = halo(planes, orb, grid)
    local = call(local_kernel, shape(count, cells), [planes, potential], flops=10**9)
    work = call(couple_kernel, shape(count, cells), [swap, local, one, two])
    rank = lax.axis_index("orb").astype(jnp.int32)
    everyone = members == orb == 8
    if everyone:
        gram, stack = gather_all(work, orb, scale, rank.reshape(1))
    else:
        blocks = gather_leading(work, rank, members)
        leading = jnp.concatenate(blocks, 0)
        gram = jnp.einsum("ic,jc->ij", leading, leading, precision=HIGH) * scale
    parts = grid_sum(gram, orb, grid)
    if not everyone:
        rest = finish_leading(work, blocks, sum(parts), rank, scale)
        return rest.reshape(count, depth, plane)
    done = call(
        finish_kernel,
        shape(depth, count, plane),
        [rank.reshape(1), *parts, stack],
        scratch=[pltpu.VMEM((total, total), jnp.float32)],
    )
    return jnp.transpose(done, (1, 0, 2))


def solution(mesh):
    return jax.shard_map(
        per_device,
        mesh=mesh,
        in_specs=(P("orb", "grid", None), P("grid", None)),
        out_specs=P("orb", "grid", None),
        check_vma=False,
    )
```

```python
import functools

import jax
import jax.numpy as jnp
from jax import lax
from jax.experimental import pallas as pl
from jax.experimental.pallas import tpu as pltpu
from jax.sharding import PartitionSpec as P

PANEL = 32
NPANEL = 2
NY = 32

COEFFS = (
    -5369.0 / 1800.0,
    12.0 / 7.0,
    -15.0 / 56.0,
    10.0 / 189.0,
    -1.0 / 112.0,
    2.0 / 1925.0,
    -1.0 / 16632.0,
)
HIGH = lax.Precision.HIGHEST
RIM = 6
LAST = 6
BOTH = ("orb", "grid")


def local_kernel(v_ref, pot_ref, out_ref):
    depth, count, plane = v_ref.shape
    lane = lax.broadcasted_iota(jnp.int32, (count, plane), 1)
    column = lane % NY
    for p in range(depth):
        here = v_ref[p]
        acc = (-1.5 * COEFFS[0] + pot_ref[p : p + 1, :]) * here
        for k in range(1, RIM + 1):
            up, down = NY * k, plane - NY * k
            near = jnp.where(lane < down, pltpu.roll(here, down, 1), 0.0)
            near += jnp.where(lane >= up, pltpu.roll(here, up, 1), 0.0)
            near += jnp.where(column + k < NY, pltpu.roll(here, plane - k, 1), 0.0)
            near += jnp.where(column >= k, pltpu.roll(here, k, 1), 0.0)
            if p + k < depth:
                near += v_ref[p + k]
            if p >= k:
                near += v_ref[p - k]
            acc += (-0.5 * COEFFS[k]) * near
        out_ref[:, p * plane : (p + 1) * plane] = acc


def couple_kernel(swap_ref, local_ref, one_ref, two_ref, out_ref):
    @pl.when(swap_ref[0] == 0)
    def _():
        couple(local_ref, one_ref, two_ref, out_ref)

    @pl.when(swap_ref[0] == 1)
    def _():
        couple(local_ref, two_ref, one_ref, out_ref)


def couple(local_ref, before_ref, after_ref, out_ref):
    rim, count, plane = before_ref.shape
    depth = out_ref.shape[1] // plane
    for p in range(depth):
        acc = local_ref[:, p * plane : (p + 1) * plane]
        for q in range(rim):
            if p + rim - q <= rim:
                acc += (-0.5 * COEFFS[p + rim - q]) * before_ref[q]
            if depth + q - p <= rim:
                acc += (-0.5 * COEFFS[depth + q - p]) * after_ref[q]
        out_ref[:, p * plane : (p + 1) * plane] = acc


def place(rank, mask, rows):
    return pl.multiple_of((rank // 2 ^ mask // 2) * rows, rows)


def store_pair(rank, mask, one_ref, two_ref, stack_ref):
    odd = rank % 2 == 1
    one, two = one_ref[...], two_ref[...]
    pair = jnp.concatenate([jnp.where(odd, two, one), jnp.where(odd, one, two)], 0)
    high = pair.astype(jnp.bfloat16)
    low = (pair - high.astype(jnp.float32)).astype(jnp.bfloat16)
    rows, half = pair.shape[0], stack_ref.shape[0] // 2
    first = place(rank, mask, rows)
    stack_ref[pl.ds(first, rows), :] = high
    stack_ref[pl.ds(half + first, rows), :] = low
    return jnp.concatenate([high, low], 0)


def products(left, right, scale):
    every = lax.dot_general(
        left, right, (((1,), (1,)), ((), ())), preferred_element_type=jnp.float32
    )
    rows, columns = left.shape[0] // 2, right.shape[0] // 2
    both = every[:rows] + every[rows:]
    return (both[:, :columns] + both[:, columns:]) * scale


def gram_kernel(scale, masks, rank_ref, *refs):
    blocks, (gram_ref, stack_ref) = refs[:-2], refs[-2:]
    rows = 2 * blocks[0].shape[0]
    half = stack_ref.shape[0] // 2
    rank = rank_ref[0]
    missing = place(rank, LAST, rows)
    blank = jnp.zeros((rows, stack_ref.shape[1]), jnp.bfloat16)
    stack_ref[pl.ds(missing, rows), :] = blank
    stack_ref[pl.ds(half + missing, rows), :] = blank
    for k, mask in enumerate(masks):
        store_pair(rank, mask, blocks[2 * k], blocks[2 * k + 1], stack_ref)
    whole = stack_ref[...]
    gram_ref[...] = products(whole, whole, scale)


def beside(gram):
    half = gram.shape[0] // 2
    return jnp.concatenate([gram[:half], gram[half:]], 1)


def last_kernel(scale, rank_ref, one_ref, two_ref, early_ref, before_ref, gram_ref, stack_ref):
    rank = rank_ref[0]
    rows = 2 * one_ref.shape[0]
    total = early_ref.shape[0]
    needed = (rank // 2 ^ LAST // 2) < rank // 2

    @pl.when(needed)
    def _():
        pair = store_pair(rank, LAST, one_ref, two_ref, stack_ref)
        lines = products(pair, stack_ref[...], scale)
        repeated = jnp.concatenate([lines] * (total // rows), 0)
        first = place(rank, LAST, rows)
        row = lax.broadcasted_iota(jnp.int32, (total, total), 0)
        column = lax.broadcasted_iota(jnp.int32, (total, total), 1)
        gram = jnp.where((column >= first) & (column < first + rows), repeated.T, early_ref[...])
        gram = jnp.where((row >= first) & (row < first + rows), repeated, gram)
        gram_ref[...] = beside(gram)

    @pl.when(jnp.logical_not(needed))
    def _():
        gram_ref[...] = beside(early_ref[...])


def invert_factor(gram, leading):
    size = gram.shape[0]
    rows = 8
    full = (rows, 2 * size)
    ident = (
        lax.broadcasted_iota(jnp.int32, (size, size), 0)
        == lax.broadcasted_iota(jnp.int32, (size, size), 1)
    ).astype(jnp.float32)
    zero = lax.broadcasted_iota(jnp.int32, full, 1).astype(jnp.float32) * 0.0
    whole = jnp.concatenate([gram, ident], 1)
    tiles = [whole[i : i + rows] for i in range(0, leading, rows)]

    def columns(i, first):
        return [jnp.broadcast_to(tiles[i][:, k : k + 1], full) for k in range(first, first + rows)]

    def spread(value, a):
        return jnp.broadcast_to(value[a : a + 1], full)

    own = [column + zero for column in columns(0, 0)]
    done = []
    for t in range(len(tiles)):
        last = t + 1 == len(tiles)
        if not last:
            after = [column + zero for column in columns(t + 1, t * rows)]
            following = [column + zero for column in columns(t + 1, (t + 1) * rows)]
        line = [spread(tiles[t], a) for a in range(rows)]
        pivot = [[spread(own[b], a) for b in range(a + 1)] for a in range(rows)]
        factor = [[None] * rows for _ in range(rows)]
        inverse = []
        for a in range(rows):
            inverse.append(1.0 / pivot[a][a])
            for b in range(a + 1, rows):
                factor[b][a] = pivot[b][a] * inverse[a]
                line[b] = line[b] - factor[b][a] * line[a]
                for c in range(a + 1, b + 1):
                    pivot[b][c] = pivot[b][c] - factor[b][a] * pivot[c][a]
        done += [(line[a] * lax.rsqrt(pivot[a][a]))[:1] for a in range(rows)]
        if last:
            break
        scaled = [line[a] * inverse[a] for a in range(rows)]
        for a in range(rows):
            tiles[t + 1] = tiles[t + 1] - after[a] * scaled[a]
            weight = after[a] * inverse[a]
            following = [f - weight * spread(after[a], c) for c, f in enumerate(following)]
            for b in range(a + 1, rows):
                after[b] = after[b] - factor[b][a] * after[a]
        for a in range(rows - 1, -1, -1):
            for b in range(a):
                scaled[b] = scaled[b] - factor[a][b] * scaled[a]
        for i in range(t + 2, len(tiles)):
            terms = [column * scaled[a] for a, column in enumerate(columns(i, t * rows))]
            while len(terms) > 1:
                terms = [terms[k] + terms[k + 1] for k in range(0, len(terms), 2)]
            tiles[i] = tiles[i] - terms[0]
        own = following
    return jnp.concatenate(done, 0)[:, size:]


def finish_kernel(rank_ref, *refs):
    parts, (stack_ref, out_ref, factor_ref) = refs[:-3], refs[-3:]
    depth, count, plane = out_ref.shape
    gram = parts[0][...]
    for part in parts[1:]:
        gram = gram + part[...]
    size = gram.shape[1] // 2
    gram = jnp.concatenate([gram[:, :size], gram[:, size:]], 0)
    held = 2 * count
    chip = rank_ref[0] // 2
    low_chip = 0
    for top in (1, 2, 3, 4):

        @pl.when((chip >= low_chip) & (chip < top))
        def _(top=top):
            factor_ref[: top * held, :] = invert_factor(gram, top * held)

        low_chip = top
    rows = factor_ref[pl.ds(pl.multiple_of(rank_ref[0] * count, count), count), :]
    high = rows.astype(jnp.bfloat16).astype(jnp.float32)
    low = rows - high
    left = jnp.concatenate(
        [jnp.concatenate([high, high], 1), jnp.concatenate([low, low], 1)], 0
    ).astype(jnp.bfloat16)
    for p in range(depth):
        both = jnp.dot(
            left, stack_ref[:, p * plane : (p + 1) * plane], preferred_element_type=jnp.float32
        )
        out_ref[p] = both[:count] + both[count:]


def call(kernel, out_shape, inputs, scratch=(), flops=0, aliases=None):
    in_specs = [
        pl.BlockSpec(memory_space=pltpu.SMEM if a.dtype == jnp.int32 else pltpu.VMEM)
        for a in inputs
    ]
    out_specs = jax.tree.map(lambda s: pl.BlockSpec(memory_space=pltpu.VMEM), out_shape)
    return pl.pallas_call(
        kernel,
        out_shape=out_shape,
        in_specs=in_specs,
        out_specs=out_specs,
        scratch_shapes=scratch,
        input_output_aliases=aliases or {},
        compiler_params=pltpu.CompilerParams(vmem_limit_bytes=32 * 2**20),
        cost_estimate=pl.CostEstimate(flops=flops, bytes_accessed=10**6, transcendentals=0),
    )(*inputs)


def rotation(peers, step):
    return [(i, (i + step) % peers) for i in range(peers)]


def partners(orb, grid, masks, core=0):
    return [
        (o * grid + g, (o ^ core) * grid + (g ^ masks[o % 2]))
        for o in range(orb)
        for g in range(grid)
    ]


def exchange(peers, mask):
    return [(i, i ^ mask) for i in range(peers)]


def shape(*dims, dtype=jnp.float32):
    return jax.ShapeDtypeStruct(dims, dtype)


def halo(planes, orb, grid):
    depth = planes.shape[0]
    if grid == 4 and depth == RIM:
        one = lax.ppermute(planes, BOTH, partners(orb, grid, (3, 1)))
        two = lax.ppermute(planes, BOTH, partners(orb, grid, (1, 3)))
        swap = (lax.axis_index("grid") + lax.axis_index("orb")) % 2
        return one, two, swap.astype(jnp.int32).reshape(1)
    before = lax.ppermute(planes[depth - RIM :], "grid", rotation(grid, 1))
    after = lax.ppermute(planes[:RIM], "grid", rotation(grid, -1))
    return before, after, jnp.zeros((1,), jnp.int32)


def grid_sum(part, orb, grid):
    if grid != 4:
        return [lax.psum(part, "grid")]
    sets = [partners(orb, grid, (k, k), 1) for k in (2, 1, 3)]
    return [part] + [lax.ppermute(part, BOTH, pairs) for pairs in sets]


def gather_all(work, orb, scale, rank):
    count, cells = work.shape
    total = orb * count
    pairs = []
    masks = (0, 2, 4, LAST)
    for mask in masks:
        block = work if mask == 0 else lax.ppermute(work, "orb", exchange(orb, mask))
        pairs.append([block, lax.ppermute(block, "orb", exchange(orb, 1))])
    outs = (shape(total, total), shape(2 * total, cells, dtype=jnp.bfloat16))
    early, before = call(
        functools.partial(gram_kernel, scale, masks[:-1]), outs, [rank, *sum(pairs[:-1], [])]
    )
    return call(
        functools.partial(last_kernel, scale),
        (shape(total // 2, 2 * total), outs[1]),
        [rank, *pairs[-1], early, before],
        aliases={4: 1},
    )


def gather_leading(work, rank, members):
    kept = [jnp.where(rank == m, work, jnp.zeros_like(work)) for m in range(members)]
    return lax.psum(kept, "orb")


def finish_leading(work, blocks, gram, rank, scale):
    count = work.shape[0]
    leading = jnp.concatenate(blocks, 0)
    total = leading.shape[0]
    inner = functools.partial(jnp.einsum, "ic,jc->ij", precision=HIGH)
    coeff = lax.psum(inner(work, leading) * scale, "grid")
    inverse = lax.linalg.triangular_solve(
        jnp.linalg.cholesky(gram), jnp.eye(total, dtype=gram.dtype), left_side=True, lower=True
    )
    first = jnp.minimum(rank * count, total - count)
    owned = lax.dynamic_slice_in_dim(inverse, first, count, 0)
    taken = jnp.dot(inner(coeff, inverse), inverse, precision=HIGH)
    member = rank * count < total
    rows = jnp.where(member, owned, -taken)
    return jnp.where(member, 0.0, work) + jnp.dot(rows, leading, precision=HIGH)


def per_device(wavefunctions, potential):
    planes = jnp.transpose(wavefunctions, (1, 0, 2))
    depth, count, plane = planes.shape
    cells = depth * plane
    orb, grid = lax.axis_size("orb"), lax.axis_size("grid")
    members = min(PANEL * NPANEL // count, orb)
    total = members * count
    scale = 1.0 / (cells * grid)
    one, two, swap = halo(planes, orb, grid)
    local = call(local_kernel, shape(count, cells), [planes, potential], flops=10**9)
    work = call(couple_kernel, shape(count, cells), [swap, local, one, two])
    rank = lax.axis_index("orb").astype(jnp.int32)
    everyone = members == orb == 8
    if everyone:
        gram, stack = gather_all(work, orb, scale, rank.reshape(1))
    else:
        blocks = gather_leading(work, rank, members)
        leading = jnp.concatenate(blocks, 0)
        gram = jnp.einsum("ic,jc->ij", leading, leading, precision=HIGH) * scale
    parts = grid_sum(gram, orb, grid)
    if not everyone:
        rest = finish_leading(work, blocks, sum(parts), rank, scale)
        return rest.reshape(count, depth, plane)
    done = call(
        finish_kernel,
        shape(depth, count, plane),
        [rank.reshape(1), *parts, stack],
        scratch=[pltpu.VMEM((total, total), jnp.float32)],
    )
    return jnp.transpose(done, (1, 0, 2))


def solution(mesh):
    return jax.shard_map(
        per_device,
        mesh=mesh,
        in_specs=(P("orb", "grid", None), P("grid", None)),
        out_specs=P("orb", "grid", None),
        check_vma=False,
    )
```
